128 devices in a mesh: dp: 8 (over y_hi, x), tensor: 16 (over z, y_lo, core).
Axes of the slice: x: 4, y: 4 (y_hi: 2, y_lo: 2; y = y_hi * 2 + y_lo), z: 4, core: 2. Of those that a mesh axis runs over, the one named last changes fastest.
Arguments:
- queries: bfloat16 [16384, 8192], P(('dp', 'tensor')), may hold values from -128 to 128
- keys: bfloat16 [16384, 512], P(('dp', 'tensor')), may hold values from -8 to 8
- values: bfloat16 [16384, 512], P(('dp', 'tensor')), may hold values from -6 to 6
- saved_out: bfloat16 [16384, 8192], P(('dp', 'tensor')), may hold values from -6 to 6
- grad_out: bfloat16 [16384, 8192], P(('dp', 'tensor')), may hold values from -24 to 24
- normed_input: bfloat16 [16384, 8192], P(('dp', 'tensor')), may hold values from -24 to 24
- subtree_end: int32 [16384], P('dp'), may hold values from 0 to 2047, as said below
Outputs:
- grad_queries: bfloat16 [16384, 8192], P(('dp', 'tensor'))
- grad_keys: bfloat16 [16384, 512], P(('dp', 'tensor'))
- grad_values: bfloat16 [16384, 512], P(('dp', 'tensor'))
- grad_wk: float32 [8192, 512], P(('dp', 'tensor'))
- grad_wv: float32 [8192, 512], P(('dp', 'tensor'))
The draws below stay inside these ranges and needn't reach their ends.
Inputs may be any that keep to these rules, and one draw needn't show every extreme that they name: Each group of 2048 tokens is a forest in pre-order: subtree_end[j] is at least j, at most the group's last position, and subtrees nest.
All inputs are finite; a program needn't handle non-finite values.
Results may differ from the reference program's by a relative error of at most 0.005.
Values may be sent and summed in bfloat16 or wider, within the bound.
A program may use at most 448 MiB of HBM per device.

```python
import math
import jax
import jax.numpy as jnp
from jax import lax

D = 8192
HQ = 64
KVH = 4
HD = 128
SEQ = 2048
TOKENS = 16384
N_DP = 8


def shared_keys(key):
    return jax.random.normal(key, (TOKENS, KVH * HD), jnp.float32)


def draw_keys(key, part):
    base = shared_keys(key)
    return base.astype(jnp.bfloat16)


def draw_queries(key, part):
    key = jax.random.fold_in(key, 11)
    return jax.random.normal(key, (TOKENS, HQ * HD), jnp.float32).astype(jnp.bfloat16)


def draw_subtree_end(key, part):
    key = jax.random.fold_in(key, 5)
    first_key, second_key = jax.random.split(key)
    onward = jax.random.randint(first_key, (SEQ, N_DP), 0, 64)
    target = jax.random.randint(second_key, (SEQ, N_DP), 0, 1 << 20)

    def deepen(depth, inputs):
        carry_on, jump = inputs
        nested = jnp.where(carry_on != 0, depth + 1, jump % (depth + 1))
        return (nested, depth)
    start = jnp.zeros((N_DP,), jnp.int32)
    unused, depths = lax.scan(deepen, start, (onward, target))
    depths = depths.T
    places = jnp.arange(SEQ, dtype=jnp.int32)
    later = (places[None, None, :] > places[None, :, None]) & (depths[:, None, :] <= depths[:, :, None])
    following = jnp.min(jnp.where(later, places[None, None, :], SEQ), axis=2)
    return (following - 1).astype(jnp.int32).reshape(TOKENS)


def raised(result, rng, source, target, shards_of, factor):
    def block_of(position):
        return (jnp.arange(result.shape[position]) // (result.shape[position] // shards_of)).reshape((-1,) + (1,) * (result.ndim - 1 - position))

    first = jax.random.permutation(rng, shards_of)[block_of(target)]
    far = (block_of(target) + shards_of // 2) % shards_of
    return jnp.where((block_of(source) == first) | (block_of(source) == far), factor * result, result)


def block_scale(rng, dims, pieces, low, top_value):
    def one(position, parts):
        steps = jax.random.uniform(jax.random.fold_in(jax.random.fold_in(rng, 6), position), (parts,), jnp.float32, low / len(pieces), top_value / len(pieces))
        return jnp.repeat(jnp.exp(steps), dims[position] // parts).reshape((-1,) + (1,) * (len(dims) - position - 1))

    loudness = one(*pieces[0])
    for cut in pieces[1:]:
        loudness = loudness * one(*cut)
    return loudness


def scatter_about(stream_key, extent, deviation, most, shards=(), kind=jnp.bfloat16):
    values = jax.random.normal(stream_key, extent, jnp.float32) * deviation
    if len(shards) > 0:
        values = block_scale(stream_key, extent, shards, -0.22, 0.18) * values
    return jnp.clip(values, min=-most, max=most).astype(kind)


def noise_with(key, dims, scale, limit, cuts, heavy, held_as=jnp.bfloat16):
    values = scale * jax.random.normal(key, dims, jnp.float32)
    if cuts:
        values = values * block_scale(key, dims, cuts, -0.22, 0.18)
    return jnp.clip(raised(values, jax.random.fold_in(key, 3), *heavy), -limit, limit).astype(held_as)


def setup_inputs(seed: int = 0) -> dict:
    key_list = jax.random.split(jax.random.key(seed), 8)
    return {
        "queries": draw_queries(jax.random.fold_in(key_list[7], 71), 0),
        "keys": draw_keys(jax.random.fold_in(key_list[7], 71), 0),
        "values": scatter_about(key_list[2], (TOKENS, KVH * HD), 1.0, 6.0, ((0, 128),)),
        "saved_out": scatter_about(key_list[3], (TOKENS, HQ * HD), 1.0, 6.0, ((0, 128),)),
        "grad_out": scatter_about(key_list[4], (TOKENS, HQ * HD), 4.0, 24.0, ((0, 128),)),
        "normed_input": noise_with(key_list[5], (TOKENS, D), 1.0, 24.0, ((0, 128),), (0, 1, 128, 5.5)),
        "subtree_end": draw_subtree_end(jax.random.fold_in(key_list[7], 71), 0),
    }


def group_grads(query_rows, key_rows, value_rows, out_rows, grad_rows, end_rows):
    head_group = HQ // KVH
    softmax_scale = HD ** -0.5
    key_heads = key_rows.astype(jnp.float32).reshape(SEQ, KVH, HD)
    value_heads = value_rows.astype(jnp.float32).reshape(SEQ, KVH, HD)
    key_place = jnp.arange(SEQ, dtype=jnp.int32)
    block = math.gcd(SEQ, 256)

    def advance(carry, block_index):
        key_sum, value_sum = carry
        first = (block_index * block).astype(jnp.int32)
        query_block = lax.dynamic_slice_in_dim(query_rows, first, block, 0).astype(jnp.float32).reshape(block, KVH, head_group, HD)
        grad_block = lax.dynamic_slice_in_dim(grad_rows, first, block, 0).astype(jnp.float32).reshape(block, KVH, head_group, HD)
        out_block = lax.dynamic_slice_in_dim(out_rows, first, block, 0).astype(jnp.float32).reshape(block, KVH, head_group, HD)
        query_place = first + jnp.arange(block, dtype=jnp.int32)
        allowed = (key_place[None, :] <= query_place[:, None]) & (query_place[:, None] <= end_rows[None, :])
        scores = jnp.einsum('rgqd,bgd->gqrb', query_block, key_heads) * softmax_scale
        highest = jnp.max(jnp.where(allowed, scores, -jnp.inf), axis=-1)
        totals = jnp.sum(jnp.where(allowed, jnp.exp(scores - highest[..., None]), 0.0), axis=-1)
        log_total = highest + jnp.log(totals)
        prob = jnp.where(allowed, jnp.exp(scores - log_total[..., None]), 0.0)
        prob_b = lax.optimization_barrier(prob.astype(jnp.bfloat16)).astype(jnp.float32)
        out_dot = jnp.einsum('rgqd,rgqd->gqr', grad_block, out_block)
        dprob = jnp.einsum('rgqd,bgd->gqrb', grad_block, value_heads)
        dscore = prob * (dprob - out_dot[..., None])
        dscore_b = lax.optimization_barrier(dscore.astype(jnp.bfloat16)).astype(jnp.float32)
        grad_query = (jnp.einsum('gqrb,bgd->rgqd', dscore_b, key_heads) * softmax_scale).astype(jnp.bfloat16)
        key_sum = key_sum + jnp.einsum('gqrb,rgqd->bgd', dscore_b, query_block) * softmax_scale
        value_sum = value_sum + jnp.einsum('gqrb,rgqd->bgd', prob_b, grad_block)
        return (key_sum, value_sum), grad_query.reshape(block, HQ * HD)

    empty = jnp.zeros((SEQ, KVH, HD), jnp.float32)
    (key_sum, value_sum), grad_blocks = lax.scan(advance, (empty, empty), jnp.arange(SEQ // block, dtype=jnp.int32))
    return (grad_blocks.reshape(SEQ, HQ * HD),
            key_sum.astype(jnp.bfloat16).reshape(SEQ, KVH * HD),
            value_sum.astype(jnp.bfloat16).reshape(SEQ, KVH * HD))


def reference(queries, keys, values, saved_out, grad_out, normed_input, subtree_end):
    def per_group(packed):
        return group_grads(*packed)

    grad_queries, grad_keys, grad_values = lax.map(per_group, (
        queries.reshape(N_DP, SEQ, HQ * HD),
        keys.reshape(N_DP, SEQ, KVH * HD),
        values.reshape(N_DP, SEQ, KVH * HD),
        saved_out.reshape(N_DP, SEQ, HQ * HD),
        grad_out.reshape(N_DP, SEQ, HQ * HD),
        subtree_end.reshape(N_DP, SEQ)))
    grad_queries = grad_queries.reshape(TOKENS, HQ * HD)
    grad_keys = grad_keys.reshape(TOKENS, KVH * HD)
    grad_values = grad_values.reshape(TOKENS, KVH * HD)
    grad_wk = jnp.dot(normed_input.T, grad_keys, preferred_element_type=jnp.float32)
    grad_wv = jnp.dot(normed_input.T, grad_values, preferred_element_type=jnp.float32)
    return (grad_queries, grad_keys, grad_values, grad_wk, grad_wv)
```

```python
import functools
import math

import jax
import jax.numpy as jnp
from jax import lax
from jax.experimental import pallas as pl
from jax.experimental.pallas import tpu as pltpu
from jax.sharding import PartitionSpec as P

D = 8192
HQ = 64
KVH = 4
HD = 128
SEQ = 2048
ROWS = 128
BLOCKS = SEQ // ROWS
HG = HQ // KVH
HB = 4
WIDTHS = (128, 256, 384, 640, SEQ - ROWS)
SCALE = HD ** (-0.5)
NT = (((1,), (1,)), ((), ()))
TN = (((0,), (0,)), ((), ()))
f32 = jnp.float32
bf16 = jnp.bfloat16


def attention_kernel(
    place_ref, end_ref, q_ref, do_ref, o_ref, k_ref, v_ref,
    dq_ref, dk_ref, dv_ref, rank, pick, bias, kc, vc,
):
    t = place_ref[0]
    g = pl.program_id(0)
    first = t * ROWS
    lane = lax.broadcasted_iota(jnp.int32, (ROWS, ROWS), 1)
    sub = lax.broadcasted_iota(jnp.int32, (ROWS, ROWS), 0)

    pos = (
        lax.broadcasted_iota(jnp.int32, (BLOCKS, ROWS), 0) * ROWS
        + lax.broadcasted_iota(jnp.int32, (BLOCKS, ROWS), 1)
    )
    far = (pos < first) & (end_ref[...] >= first)
    n_far = jnp.sum(far.astype(jnp.int32))

    @pl.when(g == 0)
    def _prepare():
        flags = far.astype(f32).astype(bf16)
        upto = (sub <= lane).astype(f32).astype(bf16)
        within = jnp.dot(flags, upto, preferred_element_type=f32)
        totals = jnp.dot(flags, jnp.ones((ROWS, ROWS), bf16), preferred_element_type=f32)
        earlier = (
            lax.broadcasted_iota(jnp.int32, (BLOCKS, BLOCKS), 1)
            < lax.broadcasted_iota(jnp.int32, (BLOCKS, BLOCKS), 0)
        )
        before = jnp.dot(
            earlier.astype(f32).astype(bf16), totals.astype(bf16), preferred_element_type=f32
        )
        rank[...] = jnp.where(far, (within + before).astype(jnp.int32) - 1, -1)
        own_end = end_ref[pl.ds(t, 1), :]
        end_col = jnp.sum(jnp.where(sub == lane, own_end, 0), axis=1, keepdims=True)
        ok = (sub <= lane) & (lane + first <= end_col)
        bias[0:ROWS, :] = jnp.where(ok, 0.0, -1e30)
        kc[0:ROWS, :] = k_ref[pl.ds(pl.multiple_of(first, ROWS), ROWS), :]
        vc[0:ROWS, :] = v_ref[pl.ds(pl.multiple_of(first, ROWS), ROWS), :]

    def run(width):
        total = width + ROWS

        @pl.when(g == 0)
        def _compact():
            def one(b, carry):
                at = pl.multiple_of(b * ROWS, ROWS)
                end_sum = jnp.zeros((ROWS, ROWS), jnp.int32)
                for r in range(BLOCKS):
                    hit = rank[r : r + 1, :] == sub + at
                    end_sum = end_sum + jnp.where(hit, end_ref[r : r + 1, :] + 1, 0)
                    pick[pl.ds(at, ROWS), r * ROWS : (r + 1) * ROWS] = hit.astype(f32).astype(bf16)
                end_col = jnp.sum(end_sum, axis=1, keepdims=True) - 1
                bias[pl.ds(at + ROWS, ROWS), :] = jnp.where(lane + first <= end_col, 0.0, -1e30)
                chosen = pick[pl.ds(at, ROWS), :]
                kc[pl.ds(at + ROWS, ROWS), :] = jnp.dot(
                    chosen, k_ref[...], preferred_element_type=f32
                ).astype(bf16)
                vc[pl.ds(at + ROWS, ROWS), :] = jnp.dot(
                    chosen, v_ref[...], preferred_element_type=f32
                ).astype(bf16)
                return carry

            lax.fori_loop(0, width // ROWS, one, 0)

        gcol = pl.multiple_of(g * HD, HD)
        kg = kc[0:total, pl.ds(gcol, HD)]
        vg = vc[0:total, pl.ds(gcol, HD)]

        def heads(i, acc):
            dk_acc, dv_acc = acc
            cols = [pl.ds(pl.multiple_of((i * HB + b) * HD, HD), HD) for b in range(HB)]
            q4 = jnp.concatenate([q_ref[:, c] for c in cols], axis=0)
            do4 = jnp.concatenate([do_ref[:, c] for c in cols], axis=0)
            o4 = jnp.concatenate([o_ref[:, c] for c in cols], axis=0)
            prod = do4.astype(f32) * o4.astype(f32)
            high = prod.astype(bf16)
            low = (prod - high.astype(f32)).astype(bf16)
            ones = jnp.ones((16, HD), bf16)
            dots = (
                lax.dot_general(ones, high, NT, preferred_element_type=f32)
                + lax.dot_general(ones, low, NT, preferred_element_type=f32)
            )[0:1, :]
            b1 = bias[0:total, :]
            b4 = jnp.concatenate([b1] * HB, axis=1)
            s = lax.dot_general(kg, q4, NT, preferred_element_type=f32) * SCALE + b4
            top = jnp.max(s, axis=0, keepdims=True)
            p = jnp.exp(s - top)
            p = p * (1.0 / jnp.sum(p, axis=0, keepdims=True))
            dp = lax.dot_general(vg, do4, NT, preferred_element_type=f32)
            ds = (p * (dp - dots)).astype(bf16)
            dq = lax.dot_general(ds, kg, TN, preferred_element_type=f32) * SCALE
            for b in range(HB):
                dq_ref[:, cols[b]] = dq[b * ROWS : (b + 1) * ROWS, :].astype(bf16)
            dk_acc = dk_acc + jnp.dot(ds, q4, preferred_element_type=f32)
            dv_acc = dv_acc + jnp.dot(p.astype(bf16), do4, preferred_element_type=f32)
            return dk_acc, dv_acc

        zero = jnp.zeros((total, HD), f32)
        dk_acc, dv_acc = lax.fori_loop(0, HG // HB, heads, (zero, zero))
        dk = (dk_acc * SCALE).astype(bf16)
        dv = dv_acc.astype(bf16)
        chosen = pick[0:width, :]
        dk_ref[...] = lax.dot_general(chosen, dk[ROWS:], TN, preferred_element_type=f32).astype(bf16)
        dv_ref[...] = lax.dot_general(chosen, dv[ROWS:], TN, preferred_element_type=f32).astype(bf16)
        dk_ref[pl.ds(pl.multiple_of(first, ROWS), ROWS), :] = dk[:ROWS]
        dv_ref[pl.ds(pl.multiple_of(first, ROWS), ROWS), :] = dv[:ROWS]

    lower = -1
    for width in WIDTHS:
        pl.when((n_far > lower) & (n_far <= width))(functools.partial(run, width))
        lower = width


def attention(queries, grad_out, saved_out, key_group, value_group, subtree_end):
    place = lax.axis_index("tensor").astype(jnp.int32).reshape(1)
    wide = pl.BlockSpec((ROWS, HG * HD), lambda g, place: (0, g))
    whole = pl.BlockSpec((SEQ, KVH * HD), lambda g, place: (0, 0))
    part = pl.BlockSpec((SEQ, HD), lambda g, place: (0, g))
    far_most = SEQ - ROWS
    return pl.pallas_call(
        attention_kernel,
        grid_spec=pltpu.PrefetchScalarGridSpec(
            num_scalar_prefetch=1,
            grid=(KVH,),
            in_specs=[
                pl.BlockSpec((BLOCKS, ROWS), lambda g, place: (0, 0)),
                wide, wide, wide, whole, whole,
            ],
            out_specs=[wide, part, part],
            scratch_shapes=[
                pltpu.VMEM((BLOCKS, ROWS), jnp.int32),
                pltpu.VMEM((far_most, SEQ), bf16),
                pltpu.VMEM((SEQ, ROWS), f32),
                pltpu.VMEM((SEQ, KVH * HD), bf16),
                pltpu.VMEM((SEQ, KVH * HD), bf16),
            ],
        ),
        out_shape=[
            jax.ShapeDtypeStruct((ROWS, HQ * HD), bf16),
            jax.ShapeDtypeStruct((SEQ, KVH * HD), bf16),
            jax.ShapeDtypeStruct((SEQ, KVH * HD), bf16),
        ],
        compiler_params=pltpu.CompilerParams(vmem_limit_bytes=56 * 1024 * 1024),
    )(place, subtree_end.reshape(BLOCKS, ROWS), queries, grad_out, saved_out, key_group, value_group)


def shards(queries, keys, values, saved_out, grad_out, normed_input, subtree_end):
    row_count = queries.shape[0]
    tensor_count = lax.axis_size("tensor")
    group_tokens = row_count * tensor_count
    key_group, value_group = (
        lax.all_gather(keys, "tensor", axis=0, tiled=True),
        lax.all_gather(values, "tensor", axis=0, tiled=True),
    )
    grad_queries, key_terms, value_terms = attention(
        queries, grad_out, saved_out, key_group, value_group, subtree_end
    )
    key_local, value_local = (
        lax.psum_scatter(key_terms, "tensor", scatter_dimension=0, tiled=True),
        lax.psum_scatter(value_terms, "tensor", scatter_dimension=0, tiled=True),
    )
    grad_keys = key_local.astype(jnp.bfloat16)
    grad_values = value_local.astype(jnp.bfloat16)
    key_group_grad = lax.all_gather(grad_keys, "tensor", axis=0, tiled=True)
    value_group_grad = lax.all_gather(grad_values, "tensor", axis=0, tiled=True)
    group_count = lax.axis_size("dp")
    feature_width = D // (group_count * tensor_count)
    split_input = normed_input.reshape(row_count, group_count, tensor_count, feature_width)
    columns = lax.all_to_all(split_input, "tensor", split_axis=2, concat_axis=0, tiled=True)
    columns = columns.reshape(group_tokens, group_count * feature_width)
    contract = (((0,), (0,)), ((), ()))
    key_weight = lax.dot_general(columns, key_group_grad, contract, preferred_element_type=f32)
    value_weight = lax.dot_general(columns, value_group_grad, contract, preferred_element_type=f32)
    key_weight = key_weight.reshape(group_count, feature_width, KVH * HD)
    value_weight = value_weight.reshape(group_count, feature_width, KVH * HD)
    summed_keys, summed_values = (
        lax.psum_scatter(key_weight, "dp", scatter_dimension=0, tiled=True),
        lax.psum_scatter(value_weight, "dp", scatter_dimension=0, tiled=True),
    )
    grad_wk = summed_keys.reshape(feature_width, KVH * HD)
    grad_wv = summed_values.reshape(feature_width, KVH * HD)
    return (grad_queries, grad_keys, grad_values, grad_wk, grad_wv)


def solution(mesh):
    rows = P(("dp", "tensor"), None)
    return jax.shard_map(
        shards, mesh=mesh, in_specs=(rows,) * 6 + (P("dp"),), out_specs=(rows,) * 5, check_vma=False
    )
```

```python
import functools

import jax
import jax.numpy as jnp
from jax import lax
from jax.experimental import pallas as pl
from jax.experimental.pallas import tpu as pltpu
from jax.sharding import PartitionSpec as P

D = 8192
HQ = 64
KVH = 4
HD = 128
SEQ = 2048
ROWS = 128
BLOCKS = SEQ // ROWS
HG = HQ // KVH
HB = 4
WIDTHS = (128, 256, 384, 640, SEQ - ROWS)
SCALE = HD ** (-0.5)
NT = (((1,), (1,)), ((), ()))
TN = (((0,), (0,)), ((), ()))
f32 = jnp.float32
bf16 = jnp.bfloat16


def attention_kernel(
    place_ref, end_ref, q_ref, do_ref, o_ref, k_ref, v_ref,
    dq_ref, dkv_ref, rank, pick, bias, kc, vc,
):
    t = place_ref[0]
    g = pl.program_id(0)
    first = t * ROWS
    lane = lax.broadcasted_iota(jnp.int32, (ROWS, ROWS), 1)
    sub = lax.broadcasted_iota(jnp.int32, (ROWS, ROWS), 0)

    pos = (
        lax.broadcasted_iota(jnp.int32, (BLOCKS, ROWS), 0) * ROWS
        + lax.broadcasted_iota(jnp.int32, (BLOCKS, ROWS), 1)
    )
    far = (pos < first) & (end_ref[...] >= first)
    n_far = jnp.sum(far.astype(jnp.int32))

    @pl.when(g == 0)
    def _prepare():
        flags = far.astype(f32).astype(bf16)
        upto = (sub <= lane).astype(f32).astype(bf16)
        within = jnp.dot(flags, upto, preferred_element_type=f32)
        totals = jnp.dot(flags, jnp.ones((ROWS, ROWS), bf16), preferred_element_type=f32)
        earlier = (
            lax.broadcasted_iota(jnp.int32, (BLOCKS, BLOCKS), 1)
            < lax.broadcasted_iota(jnp.int32, (BLOCKS, BLOCKS), 0)
        )
        before = jnp.dot(
            earlier.astype(f32).astype(bf16), totals.astype(bf16), preferred_element_type=f32
        )
        rank[...] = jnp.where(far, (within + before).astype(jnp.int32) - 1, -1)
        own_end = end_ref[pl.ds(t, 1), :]
        end_col = jnp.sum(jnp.where(sub == lane, own_end, 0), axis=1, keepdims=True)
        ok = (sub <= lane) & (lane + first <= end_col)
        bias[0:ROWS, :] = jnp.where(ok, 0.0, -1e30)
        kc[0:ROWS, :] = k_ref[pl.ds(pl.multiple_of(first, ROWS), ROWS), :]
        vc[0:ROWS, :] = v_ref[pl.ds(pl.multiple_of(first, ROWS), ROWS), :]

    def run(width):
        total = width + ROWS

        @pl.when(g == 0)
        def _compact():
            def one(b, carry):
                at = pl.multiple_of(b * ROWS, ROWS)
                end_sum = jnp.zeros((ROWS, ROWS), jnp.int32)
                for r in range(BLOCKS):
                    hit = rank[r : r + 1, :] == sub + at
                    end_sum = end_sum + jnp.where(hit, end_ref[r : r + 1, :] + 1, 0)
                    pick[pl.ds(at, ROWS), r * ROWS : (r + 1) * ROWS] = hit.astype(f32).astype(bf16)
                end_col = jnp.sum(end_sum, axis=1, keepdims=True) - 1
                bias[pl.ds(at + ROWS, ROWS), :] = jnp.where(lane + first <= end_col, 0.0, -1e30)
                chosen = pick[pl.ds(at, ROWS), :]
                kc[pl.ds(at + ROWS, ROWS), :] = jnp.dot(
                    chosen, k_ref[...], preferred_element_type=f32
                ).astype(bf16)
                vc[pl.ds(at + ROWS, ROWS), :] = jnp.dot(
                    chosen, v_ref[...], preferred_element_type=f32
                ).astype(bf16)
                return carry

            lax.fori_loop(0, width // ROWS, one, 0)

        gcol = pl.multiple_of(g * HD, HD)
        kg = kc[0:total, pl.ds(gcol, HD)]
        vg = vc[0:total, pl.ds(gcol, HD)]

        def heads(i, acc):
            dk_acc, dv_acc = acc
            cols = [pl.ds(pl.multiple_of((i * HB + b) * HD, HD), HD) for b in range(HB)]
            q4 = jnp.concatenate([q_ref[:, c] for c in cols], axis=0)
            do4 = jnp.concatenate([do_ref[:, c] for c in cols], axis=0)
            o4 = jnp.concatenate([o_ref[:, c] for c in cols], axis=0)
            prod = do4.astype(f32) * o4.astype(f32)
            high = prod.astype(bf16)
            low = (prod - high.astype(f32)).astype(bf16)
            ones = jnp.ones((16, HD), bf16)
            dots = (
                lax.dot_general(ones, high, NT, preferred_element_type=f32)
                + lax.dot_general(ones, low, NT, preferred_element_type=f32)
            )[0:1, :]
            b1 = bias[0:total, :]
            b4 = jnp.concatenate([b1] * HB, axis=1)
            s = lax.dot_general(kg, q4, NT, preferred_element_type=f32) * SCALE + b4
            top = jnp.max(s, axis=0, keepdims=True)
            p = jnp.exp(s - top)
            p = p * (1.0 / jnp.sum(p, axis=0, keepdims=True))
            dp = lax.dot_general(vg, do4, NT, preferred_element_type=f32)
            ds = (p * (dp - dots)).astype(bf16)
            dq = lax.dot_general(ds, kg, TN, preferred_element_type=f32) * SCALE
            for b in range(HB):
                dq_ref[:, cols[b]] = dq[b * ROWS : (b + 1) * ROWS, :].astype(bf16)
            dk_acc = dk_acc + jnp.dot(ds, q4, preferred_element_type=f32)
            dv_acc = dv_acc + jnp.dot(p.astype(bf16), do4, preferred_element_type=f32)
            return dk_acc, dv_acc

        zero = jnp.zeros((total, HD), f32)
        dk_acc, dv_acc = lax.fori_loop(0, HG // HB, heads, (zero, zero))
        dk = (dk_acc * SCALE).astype(bf16)
        dv = dv_acc.astype(bf16)
        chosen = pick[0:width, :]
        dkv_ref[0] = lax.dot_general(chosen, dk[ROWS:], TN, preferred_element_type=f32).astype(bf16)
        dkv_ref[1] = lax.dot_general(chosen, dv[ROWS:], TN, preferred_element_type=f32).astype(bf16)
        dkv_ref[0, pl.ds(pl.multiple_of(first, ROWS), ROWS), :] = dk[:ROWS]
        dkv_ref[1, pl.ds(pl.multiple_of(first, ROWS), ROWS), :] = dv[:ROWS]

    lower = -1
    for width in WIDTHS:
        pl.when((n_far > lower) & (n_far <= width))(functools.partial(run, width))
        lower = width


def attention(queries, grad_out, saved_out, key_group, value_group, subtree_end):
    place = lax.axis_index("tensor").astype(jnp.int32).reshape(1)
    wide = pl.BlockSpec((ROWS, HG * HD), lambda g, place: (0, g))
    whole = pl.BlockSpec((SEQ, KVH * HD), lambda g, place: (0, 0))
    part = pl.BlockSpec((2, SEQ, HD), lambda g, place: (0, 0, g))
    far_most = SEQ - ROWS
    return pl.pallas_call(
        attention_kernel,
        grid_spec=pltpu.PrefetchScalarGridSpec(
            num_scalar_prefetch=1,
            grid=(KVH,),
            in_specs=[
                pl.BlockSpec((BLOCKS, ROWS), lambda g, place: (0, 0)),
                wide, wide, wide, whole, whole,
            ],
            out_specs=[wide, part],
            scratch_shapes=[
                pltpu.VMEM((BLOCKS, ROWS), jnp.int32),
                pltpu.VMEM((far_most, SEQ), bf16),
                pltpu.VMEM((SEQ, ROWS), f32),
                pltpu.VMEM((SEQ, KVH * HD), bf16),
                pltpu.VMEM((SEQ, KVH * HD), bf16),
            ],
        ),
        out_shape=[
            jax.ShapeDtypeStruct((ROWS, HQ * HD), bf16),
            jax.ShapeDtypeStruct((2, SEQ, KVH * HD), bf16),
        ],
        compiler_params=pltpu.CompilerParams(vmem_limit_bytes=56 * 1024 * 1024),
    )(place, subtree_end.reshape(BLOCKS, ROWS), queries, grad_out, saved_out, key_group, value_group)


MESH = pl.DeviceIdType.MESH
KV = KVH * HD
HALF = KV // 2
FEAT = 2048
ORDER = (1, 3, 2)


def coords():
    d, t = lax.axis_index("dp"), lax.axis_index("tensor")
    return d // 4, d % 4, t // 4, (t // 2) % 2, t % 2


def device(yh, x, z, yl, c):
    return (yh * 4 + x, z * 4 + yl * 2 + c)


def greet(peers):
    barrier = pltpu.get_barrier_semaphore()
    for peer in peers:
        pl.semaphore_signal(barrier, inc=1, device_id=peer, device_id_type=MESH)
    pl.semaphore_wait(barrier, len(peers))


class Sender:
    def __init__(self, send_sem, recv_sem):
        self.sems, self.all = (send_sem, recv_sem), []

    def __call__(self, src, dst, peer):
        i = len(self.all)
        copy = pltpu.make_async_remote_copy(
            src_ref=src, dst_ref=dst, send_sem=self.sems[0].at[i], recv_sem=self.sems[1].at[i],
            device_id=peer, device_id_type=MESH,
        )
        copy.start()
        self.all.append(copy)
        return copy

    def finish(self):
        for copy in self.all:
            copy.wait_send()


GATHER_COPIES = 30 + 9


def gather_kernel(k_ref, v_ref, n_ref, k_all, v_all, cols, send_sem, recv_sem, local_sem):
    yh, x, z, yl, c = coords()
    y_peer = device(yh, x, z, 1 - yl, c)
    core_peer = device(yh, x, z, yl, 1 - c)
    z_peer = {d: device(yh, x, (z + d) % 4, yl, c) for d in (1, 2, 3)}
    x_peer = {d: device(yh, (x + d) % 4, z, yl, c) for d in (1, 3)}
    greet([y_peer, core_peer, *z_peer.values(), *x_peer.values()])
    send = Sender(send_sem, recv_sem)

    def rows(zz, yy):
        return pl.ds(pl.multiple_of((zz * 4 + yy * 2 + c) * ROWS, ROWS), ROWS)

    def columns(part, xx):
        return pl.ds(pl.multiple_of(part * (D // 2) + xx * 1024, 1024), 1024)

    mine = rows(z, yl)
    first = send(k_ref, k_all.at[mine], y_peer)
    k_z = {d: send(k_ref, k_all.at[mine], z_peer[d]) for d in ORDER}
    v_z = {d: send(v_ref, v_all.at[mine], z_peer[d]) for d in ORDER}
    v_y = send(v_ref, v_all.at[mine], y_peer)
    slot_of = {0: 0, 1: 1, 3: 2}
    n_x = {}
    for d in (1, 3):
        for part in (0, 1):
            n_x[d, part] = send(
                n_ref.at[:, columns(part, (x + d) % 4)],
                cols.at[slot_of[4 - d], c, :, pl.ds(part * 1024, 1024)],
                x_peer[d],
            )
    local = [
        pltpu.make_async_copy(k_ref, k_all.at[mine], local_sem.at[0]),
        pltpu.make_async_copy(v_ref, v_all.at[mine], local_sem.at[1]),
    ]
    for part in (0, 1):
        local.append(
            pltpu.make_async_copy(
                n_ref.at[:, columns(part, x)],
                cols.at[0, c, :, pl.ds(part * 1024, 1024)],
                local_sem.at[2 + part],
            )
        )
    for copy in local:
        copy.start()
    crossed = [send(k_ref, k_all.at[mine], core_peer), send(v_ref, v_all.at[mine], core_peer)]
    for part in (0, 1):
        crossed.append(
            send(
                n_ref.at[:, columns(part, x)],
                cols.at[0, c, :, pl.ds(part * 1024, 1024)],
                core_peer,
            )
        )

    def cross(whole, zz, yy):
        crossed.append(send(whole.at[rows(zz, yy)], whole.at[rows(zz, yy)], core_peer))

    first.wait_recv()
    other = rows(z, 1 - yl)
    k_yz = {d: send(k_all.at[other], k_all.at[other], z_peer[d]) for d in ORDER}
    cross(k_all, z, 1 - yl)
    v_zy = {}
    for d in ORDER:
        from_z = (z + 4 - d) % 4
        v_z[d].wait_recv()
        v_zy[d] = send(v_all.at[rows(from_z, yl)], v_all.at[rows(from_z, yl)], y_peer)
        cross(v_all, from_z, yl)
    for d in ORDER:
        k_z[d].wait_recv()
        cross(k_all, (z + 4 - d) % 4, yl)
    v_y.wait_recv()
    cross(v_all, z, 1 - yl)
    for d in (1, 3):
        for part in (0, 1):
            n_x[d, part].wait_recv()
        place = cols.at[slot_of[4 - d], c]
        crossed.append(send(place, place, core_peer))
    for d in ORDER:
        k_yz[d].wait_recv()
        cross(k_all, (z + 4 - d) % 4, 1 - yl)
    for d in ORDER:
        v_zy[d].wait_recv()
        cross(v_all, (z + 4 - d) % 4, 1 - yl)
    for copy in crossed:
        copy.wait_recv()
    for copy in local:
        copy.wait()
    send.finish()


def gather(keys, values, normed_input):
    return pl.pallas_call(
        gather_kernel,
        in_specs=[pl.BlockSpec(memory_space=pl.ANY)] * 3,
        out_specs=[pl.BlockSpec(memory_space=pl.ANY)] * 3,
        out_shape=[
            jax.ShapeDtypeStruct((SEQ, KV), bf16),
            jax.ShapeDtypeStruct((SEQ, KV), bf16),
            jax.ShapeDtypeStruct((3, 2, ROWS, FEAT), bf16),
        ],
        scratch_shapes=[
            pltpu.SemaphoreType.DMA((GATHER_COPIES,)),
            pltpu.SemaphoreType.DMA((GATHER_COPIES,)),
            pltpu.SemaphoreType.DMA((4,)),
        ],
        compiler_params=pltpu.CompilerParams(collective_id=0, has_side_effects=True),
    )(keys, values, normed_input)


SUM_COPIES = 56


def sum_kernel(
    part_ref, n_ref, cols_ref, gk_ref, gv_ref, wk_ref, wv_ref,
    cols, own, came, a1, b1, a1_in, b1_in, b2, b2_in, a2, a2_in, grads, g_in,
    wa, wb, wa_in, wb_in, wa2, wb2, wa2_in, wb2_in, w_own, w_in,
    send_sem, recv_sem, local_sem,
):
    yh, x, z, yl, c = coords()
    y = yh * 2 + yl
    y_peer = device(yh, x, z, 1 - yl, c)
    core_peer = device(yh, x, z, yl, 1 - c)
    z_at = {d: (z + d) % 4 for d in range(4)}
    y_at = {d: (y + d) % 4 for d in range(4)}
    z_peer = {d: device(yh, x, z_at[d], yl, c) for d in ORDER}
    y_ring = {d: device(y_at[d] // 2, x, z, y_at[d] % 2, c) for d in ORDER}
    x_peer = {d: device(yh, (x + d) % 4, z, yl, c) for d in ORDER}
    greet([core_peer, *z_peer.values(), *y_ring.values(), *x_peer.values()])
    send = Sender(send_sem, recv_sem)

    local, cross = {}, {}
    for i, d in enumerate((1, 3, 2, 0)):
        cross[d] = send(part_ref.at[1 - c, z_at[d]], came.at[z_at[d]], core_peer)
        local[d] = pltpu.make_async_copy(part_ref.at[c, z_at[d]], own.at[z_at[d]], local_sem.at[i])
        local[d].start()
    n_x = []
    for part in (0, 1):
        start = pl.multiple_of(part * (D // 2) + ((x + 2) % 4) * 1024, 1024)
        n_x.append(
            send(
                n_ref.at[:, pl.ds(start, 1024)],
                cols.at[2, c, :, pl.ds(part * 1024, 1024)],
                x_peer[2],
            )
        )
    loads = []
    for slot, d in ((0, 0), (1, 1), (2, 3)):
        copy = pltpu.make_async_copy(cols_ref.at[slot], cols.at[d], local_sem.at[4 + slot])
        copy.start()
        loads.append(copy)

    a_z, b_y = {}, {}
    for d in (1, 3, 2, 0):
        at = z_at[d]
        cross[d].wait_recv()
        local[d].wait()
        for yy in (0, 1):
            total = own[at, yy].astype(f32) + came[at, yy].astype(f32)
            a1[at, yy] = total[:, :HALF].astype(bf16)
            b1[at, yy] = total[:, HALF:].astype(bf16)
        if d:
            a_z[d] = send(a1.at[at], a1_in.at[d - 1], z_peer[d])
        b_y[d] = send(b1.at[at, 1 - yl], b1_in.at[at], y_peer)
    b_z = {}
    for d in ORDER:
        at = z_at[d]
        b_y[d].wait_recv()
        b2[d - 1] = (b1[at, yl].astype(f32) + b1_in[at].astype(f32)).astype(bf16)
        b_z[d] = send(b2.at[d - 1], b2_in.at[d - 1], z_peer[d])
    for d in ORDER:
        a_z[d].wait_recv()

    def left(yy):
        total = a1[z, yy].astype(f32)
        for d in ORDER:
            total = total + a1_in[d - 1, yy].astype(f32)
        return total

    a2[...] = left(1 - yl).astype(bf16)
    a_y = send(a2, a2_in, y_peer)
    kept = left(yl)
    a_y.wait_recv()
    grads[0, :, :HALF] = (kept + a2_in[...].astype(f32)).astype(bf16)
    g_x = []
    for d in ORDER:
        g_x.append(
            send(
                grads.at[0, :, pl.ds(0, HALF)], grads.at[4 - d, :, pl.ds(0, HALF)], x_peer[d]
            )
        )
    b_y[0].wait_recv()
    total = b1[z, yl].astype(f32) + b1_in[z].astype(f32)
    for d in ORDER:
        b_z[d].wait_recv()
        total = total + b2_in[d - 1].astype(f32)
    grads[0, :, HALF:] = total.astype(bf16)
    for d in ORDER:
        g_x.append(
            send(
                grads.at[0, :, pl.ds(HALF, HALF)], grads.at[4 - d, :, pl.ds(HALF, HALF)], x_peer[d]
            )
        )
    theirs = pl.ds(pl.multiple_of((1 - c) * ROWS, ROWS), ROWS)
    ours = pl.ds(pl.multiple_of(c * ROWS, ROWS), ROWS)
    g_core = send(grads.at[0, theirs], g_in, core_peer)
    for copy in n_x:
        copy.wait_recv()
    n_core = send(cols.at[2, c], cols.at[2, c], core_peer)
    g_core.wait_recv()
    is_key = c == 0
    mine, other = grads[0, ours, :].astype(f32), g_in[...].astype(f32)
    gk_ref[...] = jnp.where(is_key, mine, other).astype(bf16)
    gv_ref[...] = jnp.where(is_key, other, mine).astype(bf16)
    for copy in loads:
        copy.wait()
    n_core.wait_recv()
    for copy in g_x:
        copy.wait_recv()

    right_side = grads[...].reshape(4 * 2 * ROWS, KV)
    w_a, w_b = {}, {}
    for d in (1, 3, 2, 0):
        at = z_at[d]
        for top in (0, 1):
            start = pl.multiple_of(top * 1024 + at * 256, 256)
            left_side = cols[:, :, :, pl.ds(start, 256)].reshape(4 * 2 * ROWS, 256)
            block = lax.dot_general(left_side, right_side, TN, preferred_element_type=f32)
            block = block.astype(bf16)
            for low in (0, 1):
                piece = block[low * ROWS : (low + 1) * ROWS]
                wa[at, top * 2 + low] = piece[:, :HALF]
                wb[top * 2 + low, at] = piece[:, HALF:]
        if d:
            w_a[d] = send(wa.at[at], wa_in.at[d - 1], z_peer[d])
    for d in ORDER:
        w_b[d] = send(wb.at[y_at[d]], wb_in.at[d - 1], y_ring[d])
    for d in ORDER:
        w_a[d].wait_recv()

    def over_z(yy):
        total = wa[z, yy].astype(f32)
        for d in ORDER:
            total = total + wa_in[d - 1, yy].astype(f32)
        return total

    w_ay, w_bz = {}, {}
    for d in ORDER:
        wa2[d - 1] = over_z(y_at[d]).astype(bf16)
        w_ay[d] = send(wa2.at[d - 1], wa2_in.at[d - 1], y_ring[d])
    for d in ORDER:
        w_b[d].wait_recv()

    def over_y(zz):
        total = wb[y, zz].astype(f32)
        for d in ORDER:
            total = total + wb_in[d - 1, zz].astype(f32)
        return total

    for d in ORDER:
        wb2[d - 1] = over_y(z_at[d]).astype(bf16)
        w_bz[d] = send(wb2.at[d - 1], wb2_in.at[d - 1], z_peer[d])
    total = over_z(y)
    for d in ORDER:
        w_ay[d].wait_recv()
        total = total + wa2_in[d - 1].astype(f32)
    w_own[:, :HALF] = total
    total = over_y(z)
    for d in ORDER:
        w_bz[d].wait_recv()
        total = total + wb2_in[d - 1].astype(f32)
    w_own[:, HALF:] = total
    theirs = pl.ds(pl.multiple_of((1 - c) * 64, 64), 64)
    ours = pl.ds(pl.multiple_of(c * 64, 64), 64)
    w_core = send(w_own.at[theirs], w_in, core_peer)
    mine = w_own[ours, :]
    w_core.wait_recv()
    other = w_in[...]
    wk_ref[...] = jnp.where(is_key, mine, other)
    wv_ref[...] = jnp.where(is_key, other, mine)
    send.finish()


def sums(parts, normed_input, cols):
    vmem = lambda *shape: pltpu.VMEM(shape, bf16)
    anywhere = pl.BlockSpec(memory_space=pl.ANY)
    inside = pl.BlockSpec(memory_space=pltpu.VMEM)
    R2 = 2 * ROWS
    return pl.pallas_call(
        sum_kernel,
        in_specs=[anywhere] * 3,
        out_specs=[inside] * 4,
        out_shape=[
            jax.ShapeDtypeStruct((ROWS, KV), bf16),
            jax.ShapeDtypeStruct((ROWS, KV), bf16),
            jax.ShapeDtypeStruct((64, KV), f32),
            jax.ShapeDtypeStruct((64, KV), f32),
        ],
        scratch_shapes=[
            vmem(4, 2, ROWS, FEAT),
            vmem(4, 2, R2, KV),
            vmem(4, 2, R2, KV),
            vmem(4, 2, R2, HALF),
            vmem(4, 2, R2, HALF),
            vmem(3, 2, R2, HALF),
            vmem(4, R2, HALF),
            vmem(3, R2, HALF),
            vmem(3, R2, HALF),
            vmem(R2, HALF),
            vmem(R2, HALF),
            vmem(4, R2, KV),
            vmem(ROWS, KV),
            vmem(4, 4, ROWS, HALF),
            vmem(4, 4, ROWS, HALF),
            vmem(3, 4, ROWS, HALF),
            vmem(3, 4, ROWS, HALF),
            vmem(3, ROWS, HALF),
            vmem(3, ROWS, HALF),
            vmem(3, ROWS, HALF),
            vmem(3, ROWS, HALF),
            pltpu.VMEM((ROWS, KV), f32),
            pltpu.VMEM((64, KV), f32),
            pltpu.SemaphoreType.DMA((SUM_COPIES,)),
            pltpu.SemaphoreType.DMA((SUM_COPIES,)),
            pltpu.SemaphoreType.DMA((7,)),
        ],
        compiler_params=pltpu.CompilerParams(
            collective_id=1, has_side_effects=True, vmem_limit_bytes=48 * 1024 * 1024
        ),
    )(parts.reshape(2, 4, 2, R2, KV), normed_input, cols)


def shards(queries, keys, values, saved_out, grad_out, normed_input, subtree_end):
    key_group, value_group, cols = gather(keys, values, normed_input)
    grad_queries, parts = attention(
        queries, grad_out, saved_out, key_group, value_group, subtree_end
    )
    return (grad_queries, *sums(parts, normed_input, cols))


def solution(mesh):
    rows = P(("dp", "tensor"), None)
    return jax.shard_map(
        shards, mesh=mesh, in_specs=(rows,) * 6 + (P("dp"),), out_specs=(rows,) * 5, check_vma=False
    )
```

```python
import functools

import jax
import jax.numpy as jnp
from jax import lax
from jax.experimental import pallas as pl
from jax.experimental.pallas import tpu as pltpu
from jax.sharding import PartitionSpec as P

D = 8192
HQ = 64
KVH = 4
HD = 128
SEQ = 2048
ROWS = 128
BLOCKS = SEQ // ROWS
HG = HQ // KVH
HB = 8
WIDTHS = (128, 256, 384, 512, 640, SEQ - ROWS)
SCALE = HD ** (-0.5)
LOG2E = 1.4426950408889634
NT = (((1,), (1,)), ((), ()))
TN = (((0,), (0,)), ((), ()))
f32 = jnp.float32
bf16 = jnp.bfloat16


def attention_kernel(
    place_ref, end_ref, q_ref, do_ref, o_ref, k_ref, v_ref,
    dq_ref, dkv_ref, rank, pick, put, bias, kc, vc,
):
    t = place_ref[0]
    g = pl.program_id(0)
    first = t * ROWS
    lane = lax.broadcasted_iota(jnp.int32, (ROWS, ROWS), 1)
    sub = lax.broadcasted_iota(jnp.int32, (ROWS, ROWS), 0)

    pos = (
        lax.broadcasted_iota(jnp.int32, (BLOCKS, ROWS), 0) * ROWS
        + lax.broadcasted_iota(jnp.int32, (BLOCKS, ROWS), 1)
    )
    far = (pos < first) & (end_ref[...] >= first)
    n_far = jnp.sum(far.astype(jnp.int32))

    @pl.when(g == 0)
    def _prepare():
        flags = far.astype(f32).astype(bf16)
        upto = (sub <= lane).astype(f32).astype(bf16)
        within = jnp.dot(flags, upto, preferred_element_type=f32)
        totals = jnp.dot(flags, jnp.ones((ROWS, ROWS), bf16), preferred_element_type=f32)
        earlier = (
            lax.broadcasted_iota(jnp.int32, (BLOCKS, BLOCKS), 1)
            < lax.broadcasted_iota(jnp.int32, (BLOCKS, BLOCKS), 0)
        )
        before = jnp.dot(
            earlier.astype(f32).astype(bf16), totals.astype(bf16), preferred_element_type=f32
        )
        rank[...] = jnp.where(far, (within + before).astype(jnp.int32) - 1, -1)
        own_end = end_ref[pl.ds(t, 1), :]
        end_col = jnp.sum(jnp.where(sub == lane, own_end, 0), axis=1, keepdims=True)
        ok = (sub <= lane) & (lane + first <= end_col)
        bias[0:ROWS, :] = jnp.where(ok, 0.0, -1e30)
        kc[0:ROWS, :] = k_ref[pl.ds(pl.multiple_of(first, ROWS), ROWS), :]
        vc[0:ROWS, :] = v_ref[pl.ds(pl.multiple_of(first, ROWS), ROWS), :]

    def run(width):
        total = width + ROWS

        @pl.when(g == 0)
        def _compact():
            def one(b, carry):
                at = pl.multiple_of(b * ROWS, ROWS)
                end_sum = jnp.zeros((ROWS, ROWS), jnp.int32)
                for r in range(BLOCKS):
                    column = jnp.sum(
                        jnp.where(sub == lane, rank[r : r + 1, :], 0), axis=1, keepdims=True
                    )
                    put[r * ROWS : (r + 1) * ROWS, pl.ds(at, ROWS)] = (
                        (column == lane + at).astype(f32).astype(bf16)
                    )
                    hit = rank[r : r + 1, :] == sub + at
                    end_sum = end_sum + jnp.where(hit, end_ref[r : r + 1, :] + 1, 0)
                    pick[pl.ds(at, ROWS), r * ROWS : (r + 1) * ROWS] = hit.astype(f32).astype(bf16)
                end_col = jnp.sum(end_sum, axis=1, keepdims=True) - 1
                bias[pl.ds(at + ROWS, ROWS), :] = jnp.where(lane + first <= end_col, 0.0, -1e30)
                chosen = pick[pl.ds(at, ROWS), :]
                kc[pl.ds(at + ROWS, ROWS), :] = jnp.dot(
                    chosen, k_ref[...], preferred_element_type=f32
                ).astype(bf16)
                vc[pl.ds(at + ROWS, ROWS), :] = jnp.dot(
                    chosen, v_ref[...], preferred_element_type=f32
                ).astype(bf16)
                return carry

            lax.fori_loop(0, width // ROWS, one, 0)

        gcol = pl.multiple_of(g * HD, HD)
        kg = kc[0:total, pl.ds(gcol, HD)]
        vg = vc[0:total, pl.ds(gcol, HD)]

        def heads(i, acc):
            dk_acc, dv_acc = acc
            cols = [pl.ds(pl.multiple_of((i * HB + b) * HD, HD), HD) for b in range(HB)]
            q4 = jnp.concatenate([q_ref[:, c] for c in cols], axis=0)
            do4 = jnp.concatenate([do_ref[:, c] for c in cols], axis=0)
            o4 = jnp.concatenate([o_ref[:, c] for c in cols], axis=0)
            prod = do4.astype(f32) * o4.astype(f32)
            high = prod.astype(bf16)
            low = (prod - high.astype(f32)).astype(bf16)
            ones = jnp.ones((16, HD), bf16)
            dots = (
                lax.dot_general(ones, high, NT, preferred_element_type=f32)
                + lax.dot_general(ones, low, NT, preferred_element_type=f32)
            )[0:1, :]
            b1 = bias[0:total, :]
            b4 = jnp.concatenate([b1] * HB, axis=1)
            s = lax.dot_general(kg, q4, NT, preferred_element_type=f32) * (SCALE * LOG2E) + b4
            top = jnp.max(s, axis=0, keepdims=True)
            p = jnp.exp2(s - top)
            p = p * (1.0 / jnp.sum(p, axis=0, keepdims=True))
            dp = lax.dot_general(vg, do4, NT, preferred_element_type=f32)
            ds = (p * (dp - dots)).astype(bf16)
            dq = lax.dot_general(ds, kg, TN, preferred_element_type=f32) * SCALE
            for b in range(HB):
                dq_ref[:, cols[b]] = dq[b * ROWS : (b + 1) * ROWS, :].astype(bf16)
            dk_acc = dk_acc + jnp.dot(ds, q4, preferred_element_type=f32)
            dv_acc = dv_acc + jnp.dot(p.astype(bf16), do4, preferred_element_type=f32)
            return dk_acc, dv_acc

        zero = jnp.zeros((total, HD), f32)
        dk_acc, dv_acc = lax.fori_loop(0, HG // HB, heads, (zero, zero))
        dk = (dk_acc * SCALE).astype(bf16)
        dv = dv_acc.astype(bf16)
        spread = jnp.dot(
            put[:, 0:width],
            jnp.concatenate([dk[ROWS:], dv[ROWS:]], axis=1),
            preferred_element_type=f32,
        ).astype(bf16)
        dkv_ref[0] = spread[:, :HD]
        dkv_ref[1] = spread[:, HD:]
        dkv_ref[0, pl.ds(pl.multiple_of(first, ROWS), ROWS), :] = dk[:ROWS]
        dkv_ref[1, pl.ds(pl.multiple_of(first, ROWS), ROWS), :] = dv[:ROWS]

    lower = -1
    for width in WIDTHS:
        pl.when((n_far > lower) & (n_far <= width))(functools.partial(run, width))
        lower = width


def attention(queries, grad_out, saved_out, key_group, value_group, subtree_end):
    place = lax.axis_index("tensor").astype(jnp.int32).reshape(1)
    wide = pl.BlockSpec((ROWS, HG * HD), lambda g, place: (0, g))
    whole = pl.BlockSpec((SEQ, KVH * HD), lambda g, place: (0, 0))
    part = pl.BlockSpec((2, SEQ, HD), lambda g, place: (0, 0, g))
    far_most = SEQ - ROWS
    return pl.pallas_call(
        attention_kernel,
        grid_spec=pltpu.PrefetchScalarGridSpec(
            num_scalar_prefetch=1,
            grid=(KVH,),
            in_specs=[
                pl.BlockSpec((BLOCKS, ROWS), lambda g, place: (0, 0)),
                wide, wide, wide, whole, whole,
            ],
            out_specs=[wide, part],
            scratch_shapes=[
                pltpu.VMEM((BLOCKS, ROWS), jnp.int32),
                pltpu.VMEM((far_most, SEQ), bf16),
                pltpu.VMEM((SEQ, far_most), bf16),
                pltpu.VMEM((SEQ, ROWS), f32),
                pltpu.VMEM((SEQ, KVH * HD), bf16),
                pltpu.VMEM((SEQ, KVH * HD), bf16),
            ],
        ),
        out_shape=[
            jax.ShapeDtypeStruct((ROWS, HQ * HD), bf16),
            jax.ShapeDtypeStruct((2, SEQ, KVH * HD), bf16),
        ],
        compiler_params=pltpu.CompilerParams(vmem_limit_bytes=56 * 1024 * 1024),
    )(place, subtree_end.reshape(BLOCKS, ROWS), queries, grad_out, saved_out, key_group, value_group)


MESH = pl.DeviceIdType.MESH
KV = KVH * HD
FEAT = 2048
ORDER = (1, 3, 2)


def coords():
    d, t = lax.axis_index("dp"), lax.axis_index("tensor")
    return d // 4, d % 4, t // 4, (t // 2) % 2, t % 2


def device(yh, x, z, yl, c):
    return (yh * 4 + x, z * 4 + yl * 2 + c)


def greet(peers):
    barrier = pltpu.get_barrier_semaphore()
    for peer in peers:
        pl.semaphore_signal(barrier, inc=1, device_id=peer, device_id_type=MESH)
    pl.semaphore_wait(barrier, len(peers))


class Sender:
    def __init__(self, send_sem, recv_sem):
        self.sems, self.all = (send_sem, recv_sem), []

    def __call__(self, src, dst, peer):
        i = len(self.all)
        copy = pltpu.make_async_remote_copy(
            src_ref=src, dst_ref=dst, send_sem=self.sems[0].at[i], recv_sem=self.sems[1].at[i],
            device_id=peer, device_id_type=MESH,
        )
        copy.start()
        self.all.append(copy)
        return copy

    def finish(self):
        for copy in self.all:
            copy.wait_send()


GATHER_COPIES = 42


def gather_kernel(k_ref, v_ref, n_ref, k_all, v_all, cols, send_sem, recv_sem, local_sem):
    yh, x, z, yl, c = coords()
    y_peer = device(yh, x, z, 1 - yl, c)
    core_peer = device(yh, x, z, yl, 1 - c)
    z_peer = {d: device(yh, x, (z + d) % 4, yl, c) for d in (1, 2, 3)}
    x_peer = {d: device(yh, (x + d) % 4, z, yl, c) for d in ORDER}
    greet([y_peer, core_peer, *z_peer.values(), *x_peer.values()])
    send = Sender(send_sem, recv_sem)

    def rows(zz, yy):
        return pl.ds(pl.multiple_of((zz * 4 + yy * 2 + c) * ROWS, ROWS), ROWS)

    def columns(part, xx):
        return pl.ds(pl.multiple_of(part * (D // 2) + xx * 1024, 1024), 1024)

    mine = rows(z, yl)
    first = send(k_ref, k_all.at[mine], y_peer)
    k_z = {d: send(k_ref, k_all.at[mine], z_peer[d]) for d in ORDER}
    v_z = {d: send(v_ref, v_all.at[mine], z_peer[d]) for d in ORDER}
    v_y = send(v_ref, v_all.at[mine], y_peer)
    n_x = {}
    for d in ORDER:
        for part in (0, 1):
            n_x[d, part] = send(
                n_ref.at[:, columns(part, (x + d) % 4)],
                cols.at[4 - d, c, :, pl.ds(part * 1024, 1024)],
                x_peer[d],
            )
    local = [
        pltpu.make_async_copy(k_ref, k_all.at[mine], local_sem.at[0]),
        pltpu.make_async_copy(v_ref, v_all.at[mine], local_sem.at[1]),
    ]
    for part in (0, 1):
        local.append(
            pltpu.make_async_copy(
                n_ref.at[:, columns(part, x)],
                cols.at[0, c, :, pl.ds(part * 1024, 1024)],
                local_sem.at[2 + part],
            )
        )
    for copy in local:
        copy.start()
    crossed = [send(k_ref, k_all.at[mine], core_peer), send(v_ref, v_all.at[mine], core_peer)]
    for part in (0, 1):
        crossed.append(
            send(
                n_ref.at[:, columns(part, x)],
                cols.at[0, c, :, pl.ds(part * 1024, 1024)],
                core_peer,
            )
        )

    def cross(whole, zz, yy):
        crossed.append(send(whole.at[rows(zz, yy)], whole.at[rows(zz, yy)], core_peer))

    first.wait_recv()
    other = rows(z, 1 - yl)
    k_yz = {d: send(k_all.at[other], k_all.at[other], z_peer[d]) for d in ORDER}
    cross(k_all, z, 1 - yl)
    v_zy = {}
    for d in ORDER:
        from_z = (z + 4 - d) % 4
        v_z[d].wait_recv()
        v_zy[d] = send(v_all.at[rows(from_z, yl)], v_all.at[rows(from_z, yl)], y_peer)
        cross(v_all, from_z, yl)
    for d in ORDER:
        k_z[d].wait_recv()
        cross(k_all, (z + 4 - d) % 4, yl)
    v_y.wait_recv()
    cross(v_all, z, 1 - yl)
    for d in ORDER:
        k_yz[d].wait_recv()
        cross(k_all, (z + 4 - d) % 4, 1 - yl)
    for d in ORDER:
        v_zy[d].wait_recv()
        cross(v_all, (z + 4 - d) % 4, 1 - yl)
    for d in ORDER:
        for part in (0, 1):
            n_x[d, part].wait_recv()
        place = cols.at[4 - d, c]
        crossed.append(send(place, place, core_peer))
    for copy in crossed:
        copy.wait_recv()
    for copy in local:
        copy.wait()
    send.finish()


def gather(keys, values, normed_input):
    return pl.pallas_call(
        gather_kernel,
        in_specs=[pl.BlockSpec(memory_space=pl.ANY)] * 3,
        out_specs=[pl.BlockSpec(memory_space=pl.ANY)] * 3,
        out_shape=[
            jax.ShapeDtypeStruct((SEQ, KV), bf16),
            jax.ShapeDtypeStruct((SEQ, KV), bf16),
            jax.ShapeDtypeStruct((4, 2, ROWS, FEAT), bf16),
        ],
        scratch_shapes=[
            pltpu.SemaphoreType.DMA((GATHER_COPIES,)),
            pltpu.SemaphoreType.DMA((GATHER_COPIES,)),
            pltpu.SemaphoreType.DMA((4,)),
        ],
        compiler_params=pltpu.CompilerParams(collective_id=0, has_side_effects=True),
    )(keys, values, normed_input)


SUM_COPIES = 80
PARTS = 2
WIDE = KV // PARTS
HALF = WIDE // 2
SOON = (1, 3, 2, 0)


def sum_kernel(
    part_ref, cols_ref, gk_ref, gv_ref, wk_ref, wv_ref,
    cols, own, came, a1, b1, a1_in, b1_in, b2, b2_in, a2, a2_in, grads, g_in,
    wa, wb, wa_in, wb_in, wa2, wb2, wa2_in, wb2_in, w_own, w_in,
    send_sem, recv_sem, local_sem,
):
    yh, x, z, yl, c = coords()
    y = yh * 2 + yl
    y_peer = device(yh, x, z, 1 - yl, c)
    core_peer = device(yh, x, z, yl, 1 - c)
    z_at = {d: (z + d) % 4 for d in range(4)}
    y_at = {d: (y + d) % 4 for d in range(4)}
    z_peer = {d: device(yh, x, z_at[d], yl, c) for d in ORDER}
    y_ring = {d: device(y_at[d] // 2, x, z, y_at[d] % 2, c) for d in ORDER}
    x_peer = {d: device(yh, (x + d) % 4, z, yl, c) for d in ORDER}
    greet([core_peer, *z_peer.values(), *y_ring.values(), *x_peer.values()])
    send = Sender(send_sem, recv_sem)
    is_key = c == 0
    theirs = pl.ds(pl.multiple_of((1 - c) * ROWS, ROWS), ROWS)
    ours = pl.ds(pl.multiple_of(c * ROWS, ROWS), ROWS)
    local, cross, a_z, b_y, b_z, a_y, g_x = {}, {}, {}, {}, {}, {}, {}
    w_a, w_b, w_ay, w_bz = {}, {}, {}, {}

    for i, d in enumerate(SOON):
        local[d] = pltpu.make_async_copy(part_ref.at[c, z_at[d]], own.at[z_at[d]], local_sem.at[i])
        local[d].start()
    for h in range(PARTS):
        for d in SOON:
            strip = pl.ds(h * WIDE, WIDE)
            cross[h, d] = send(
                part_ref.at[1 - c, z_at[d], :, :, strip],
                came.at[z_at[d], :, :, strip],
                core_peer,
            )
    brought = pltpu.make_async_copy(cols_ref, cols, local_sem.at[4])
    brought.start()

    def scatter(h):
        for d in SOON:
            at = z_at[d]
            cross[h, d].wait_recv()
            if h == 0:
                local[d].wait()
            for yy in (0, 1):
                strip = slice(h * WIDE, (h + 1) * WIDE)
                total = own[at, yy, :, strip].astype(f32) + came[at, yy, :, strip].astype(f32)
                a1[h, at, yy] = total[:, :HALF].astype(bf16)
                b1[h, at, yy] = total[:, HALF:].astype(bf16)
            if d:
                a_z[h, d] = send(a1.at[h, at], a1_in.at[h, d - 1], z_peer[d])
            b_y[h, d] = send(b1.at[h, at, 1 - yl], b1_in.at[h, at], y_peer)

    def right_turn(h):
        for d in ORDER:
            at = z_at[d]
            b_y[h, d].wait_recv()
            b2[h, d - 1] = (b1[h, at, yl].astype(f32) + b1_in[h, at].astype(f32)).astype(bf16)
            b_z[h, d] = send(b2.at[h, d - 1], b2_in.at[h, d - 1], z_peer[d])

    def left(h, yy):
        total = a1[h, z, yy].astype(f32)
        for d in ORDER:
            total = total + a1_in[h, d - 1, yy].astype(f32)
        return total

    def left_turn(h):
        for d in ORDER:
            a_z[h, d].wait_recv()
        a2[h] = left(h, 1 - yl).astype(bf16)
        a_y[h] = send(a2.at[h], a2_in.at[h], y_peer)

    def spread(h):
        b_y[h, 0].wait_recv()
        total = b1[h, z, yl].astype(f32) + b1_in[h, z].astype(f32)
        for d in ORDER:
            b_z[h, d].wait_recv()
            total = total + b2_in[h, d - 1].astype(f32)
        grads[h, 0, :, HALF:] = total.astype(bf16)
        kept = left(h, yl)
        a_y[h].wait_recv()
        grads[h, 0, :, :HALF] = (kept + a2_in[h].astype(f32)).astype(bf16)
        for d in ORDER:
            g_x[h, d] = send(grads.at[h, 0], grads.at[h, 4 - d], x_peer[d])
        g_x[h, 0] = send(grads.at[h, 0, theirs], g_in.at[h], core_peer)

    def first_outputs():
        for h in range(PARTS):
            g_x[h, 0].wait_recv()
            mine, other = grads[h, 0, ours, :].astype(f32), g_in[h].astype(f32)
            strip = slice(h * WIDE, (h + 1) * WIDE)
            gk_ref[:, strip] = jnp.where(is_key, mine, other).astype(bf16)
            gv_ref[:, strip] = jnp.where(is_key, other, mine).astype(bf16)

    def project(h):
        for d in ORDER:
            g_x[h, d].wait_recv()
        if h == 0:
            brought.wait()
        right_side = grads[h].reshape(4 * 2 * ROWS, WIDE)
        for d in SOON:
            at = z_at[d]
            for top in (0, 1):
                start = pl.multiple_of(top * 1024 + at * 256, 256)
                left_side = cols[:, :, :, pl.ds(start, 256)].reshape(4 * 2 * ROWS, 256)
                block = lax.dot_general(left_side, right_side, TN, preferred_element_type=f32)
                block = block.astype(bf16)
                for low in (0, 1):
                    piece = block[low * ROWS : (low + 1) * ROWS]
                    wa[h, at, top * 2 + low] = piece[:, :HALF]
                    wb[h, top * 2 + low, at] = piece[:, HALF:]
            if d:
                w_a[h, d] = send(wa.at[h, at], wa_in.at[h, d - 1], z_peer[d])
        for d in ORDER:
            w_b[h, d] = send(wb.at[h, y_at[d]], wb_in.at[h, d - 1], y_ring[d])

    def over_z(h, yy):
        total = wa[h, z, yy].astype(f32)
        for d in ORDER:
            total = total + wa_in[h, d - 1, yy].astype(f32)
        return total

    def over_y(h, zz):
        total = wb[h, y, zz].astype(f32)
        for d in ORDER:
            total = total + wb_in[h, d - 1, zz].astype(f32)
        return total

    def turn(h):
        for d in ORDER:
            w_a[h, d].wait_recv()
        for d in ORDER:
            wa2[h, d - 1] = over_z(h, y_at[d]).astype(bf16)
            w_ay[h, d] = send(wa2.at[h, d - 1], wa2_in.at[h, d - 1], y_ring[d])
        for d in ORDER:
            w_b[h, d].wait_recv()
        for d in ORDER:
            wb2[h, d - 1] = over_y(h, z_at[d]).astype(bf16)
            w_bz[h, d] = send(wb2.at[h, d - 1], wb2_in.at[h, d - 1], z_peer[d])

    w_core = {}

    def finish(h):
        total = over_z(h, y)
        for d in ORDER:
            w_ay[h, d].wait_recv()
            total = total + wa2_in[h, d - 1].astype(f32)
        w_own[h, :, :HALF] = total
        total = over_y(h, z)
        for d in ORDER:
            w_bz[h, d].wait_recv()
            total = total + wb2_in[h, d - 1].astype(f32)
        w_own[h, :, HALF:] = total
        out = pl.ds(pl.multiple_of((1 - c) * 64, 64), 64)
        w_core[h] = send(w_own.at[h, out], w_in.at[h], core_peer)

    def last_outputs(h):
        mine = w_own[h, pl.ds(pl.multiple_of(c * 64, 64), 64), :]
        w_core[h].wait_recv()
        other = w_in[h]
        strip = slice(h * WIDE, (h + 1) * WIDE)
        wk_ref[:, strip] = jnp.where(is_key, mine, other)
        wv_ref[:, strip] = jnp.where(is_key, other, mine)

    scatter(0)
    right_turn(0)
    scatter(1)
    left_turn(0)
    spread(0)
    right_turn(1)
    left_turn(1)
    spread(1)
    first_outputs()
    for step in (project, turn, finish):
        for h in range(PARTS):
            step(h)
    for h in range(PARTS):
        last_outputs(h)
    send.finish()


def sums(parts, cols):
    vmem = lambda *shape: pltpu.VMEM(shape, bf16)
    anywhere = pl.BlockSpec(memory_space=pl.ANY)
    inside = pl.BlockSpec(memory_space=pltpu.VMEM)
    R2 = 2 * ROWS
    return pl.pallas_call(
        sum_kernel,
        in_specs=[anywhere] * 2,
        out_specs=[inside] * 4,
        out_shape=[
            jax.ShapeDtypeStruct((ROWS, KV), bf16),
            jax.ShapeDtypeStruct((ROWS, KV), bf16),
            jax.ShapeDtypeStruct((64, KV), f32),
            jax.ShapeDtypeStruct((64, KV), f32),
        ],
        scratch_shapes=[
            vmem(4, 2, ROWS, FEAT),
            vmem(4, 2, R2, KV),
            vmem(4, 2, R2, KV),
            vmem(PARTS, 4, 2, R2, HALF),
            vmem(PARTS, 4, 2, R2, HALF),
            vmem(PARTS, 3, 2, R2, HALF),
            vmem(PARTS, 4, R2, HALF),
            vmem(PARTS, 3, R2, HALF),
            vmem(PARTS, 3, R2, HALF),
            vmem(PARTS, R2, HALF),
            vmem(PARTS, R2, HALF),
            vmem(PARTS, 4, R2, WIDE),
            vmem(PARTS, ROWS, WIDE),
            vmem(PARTS, 4, 4, ROWS, HALF),
            vmem(PARTS, 4, 4, ROWS, HALF),
            vmem(PARTS, 3, 4, ROWS, HALF),
            vmem(PARTS, 3, 4, ROWS, HALF),
            vmem(PARTS, 3, ROWS, HALF),
            vmem(PARTS, 3, ROWS, HALF),
            vmem(PARTS, 3, ROWS, HALF),
            vmem(PARTS, 3, ROWS, HALF),
            pltpu.VMEM((PARTS, ROWS, WIDE), f32),
            pltpu.VMEM((PARTS, 64, WIDE), f32),
            pltpu.SemaphoreType.DMA((SUM_COPIES,)),
            pltpu.SemaphoreType.DMA((SUM_COPIES,)),
            pltpu.SemaphoreType.DMA((5,)),
        ],
        compiler_params=pltpu.CompilerParams(
            collective_id=1, has_side_effects=True, vmem_limit_bytes=48 * 1024 * 1024
        ),
    )(parts.reshape(2, 4, 2, R2, KV), cols)


def shards(queries, keys, values, saved_out, grad_out, normed_input, subtree_end):
    key_group, value_group, cols = gather(keys, values, normed_input)
    grad_queries, parts = attention(
        queries, grad_out, saved_out, key_group, value_group, subtree_end
    )
    return (grad_queries, *sums(parts, cols))


def solution(mesh):
    rows = P(("dp", "tensor"), None)
    return jax.shard_map(
        shards, mesh=mesh, in_specs=(rows,) * 6 + (P("dp"),), out_specs=(rows,) * 5, check_vma=False
    )
```

```python
import functools

import jax
import jax.numpy as jnp
from jax import lax
from jax.experimental import pallas as pl
from jax.experimental.pallas import tpu as pltpu
from jax.sharding import PartitionSpec as P

D = 8192
HQ = 64
KVH = 4
HD = 128
SEQ = 2048
ROWS = 128
BLOCKS = SEQ // ROWS
HG = HQ // KVH
HB = 8
WIDTHS = (128, 256, 384, 512, 640, SEQ - ROWS)
SCALE = HD ** (-0.5)
LOG2E = 1.4426950408889634
NT = (((1,), (1,)), ((), ()))
TN = (((0,), (0,)), ((), ()))
f32 = jnp.float32
bf16 = jnp.bfloat16


def attention_kernel(
    place_ref, end_ref, q_ref, do_ref, o_ref, k_ref, v_ref,
    dq_ref, dkv_ref, rank, pick, put, bias, kc, vc,
):
    t = place_ref[0]
    g = pl.program_id(0)
    first = t * ROWS
    lane = lax.broadcasted_iota(jnp.int32, (ROWS, ROWS), 1)
    sub = lax.broadcasted_iota(jnp.int32, (ROWS, ROWS), 0)

    pos = (
        lax.broadcasted_iota(jnp.int32, (BLOCKS, ROWS), 0) * ROWS
        + lax.broadcasted_iota(jnp.int32, (BLOCKS, ROWS), 1)
    )
    far = (pos < first) & (end_ref[...] >= first)
    n_far = jnp.sum(far.astype(jnp.int32))

    @pl.when(g == 0)
    def _prepare():
        flags = far.astype(f32).astype(bf16)
        upto = (sub <= lane).astype(f32).astype(bf16)
        within = jnp.dot(flags, upto, preferred_element_type=f32)
        totals = jnp.dot(flags, jnp.ones((ROWS, ROWS), bf16), preferred_element_type=f32)
        earlier = (
            lax.broadcasted_iota(jnp.int32, (BLOCKS, BLOCKS), 1)
            < lax.broadcasted_iota(jnp.int32, (BLOCKS, BLOCKS), 0)
        )
        before = jnp.dot(
            earlier.astype(f32).astype(bf16), totals.astype(bf16), preferred_element_type=f32
        )
        rank[...] = jnp.where(far, (within + before).astype(jnp.int32) - 1, -1)
        own_end = end_ref[pl.ds(t, 1), :]
        end_col = jnp.sum(jnp.where(sub == lane, own_end, 0), axis=1, keepdims=True)
        ok = (sub <= lane) & (lane + first <= end_col)
        bias[0:ROWS, :] = jnp.where(ok, 0.0, -1e30)
        kc[0:ROWS, :] = k_ref[pl.ds(pl.multiple_of(first, ROWS), ROWS), :]
        vc[0:ROWS, :] = v_ref[pl.ds(pl.multiple_of(first, ROWS), ROWS), :]

    def run(width):
        total = width + ROWS

        @pl.when(g == 0)
        def _compact():
            def one(b, carry):
                at = pl.multiple_of(b * ROWS, ROWS)
                end_sum = jnp.zeros((ROWS, ROWS), jnp.int32)
                for r in range(BLOCKS):
                    column = jnp.sum(
                        jnp.where(sub == lane, rank[r : r + 1, :], 0), axis=1, keepdims=True
                    )
                    put[r * ROWS : (r + 1) * ROWS, pl.ds(at, ROWS)] = (
                        (column == lane + at).astype(f32).astype(bf16)
                    )
                    hit = rank[r : r + 1, :] == sub + at
                    end_sum = end_sum + jnp.where(hit, end_ref[r : r + 1, :] + 1, 0)
                    pick[pl.ds(at, ROWS), r * ROWS : (r + 1) * ROWS] = hit.astype(f32).astype(bf16)
                end_col = jnp.sum(end_sum, axis=1, keepdims=True) - 1
                bias[pl.ds(at + ROWS, ROWS), :] = jnp.where(lane + first <= end_col, 0.0, -1e30)
                chosen = pick[pl.ds(at, ROWS), :]
                kc[pl.ds(at + ROWS, ROWS), :] = jnp.dot(
                    chosen, k_ref[...], preferred_element_type=f32
                ).astype(bf16)
                vc[pl.ds(at + ROWS, ROWS), :] = jnp.dot(
                    chosen, v_ref[...], preferred_element_type=f32
                ).astype(bf16)
                return carry

            lax.fori_loop(0, width // ROWS, one, 0)

        gcol = pl.multiple_of(g * HD, HD)
        kg = kc[0:total, pl.ds(gcol, HD)]
        vg = vc[0:total, pl.ds(gcol, HD)]

        def heads(i, acc):
            dk_acc, dv_acc = acc
            cols = [pl.ds(pl.multiple_of((i * HB + b) * HD, HD), HD) for b in range(HB)]
            q4 = jnp.concatenate([q_ref[:, c] for c in cols], axis=0)
            do4 = jnp.concatenate([do_ref[:, c] for c in cols], axis=0)
            o4 = jnp.concatenate([o_ref[:, c] for c in cols], axis=0)
            prod = do4.astype(f32) * o4.astype(f32)
            high = prod.astype(bf16)
            low = (prod - high.astype(f32)).astype(bf16)
            ones = jnp.ones((16, HD), bf16)
            dots = (
                lax.dot_general(ones, high, NT, preferred_element_type=f32)
                + lax.dot_general(ones, low, NT, preferred_element_type=f32)
            )[0:1, :]
            b1 = bias[0:total, :]
            b4 = jnp.concatenate([b1] * HB, axis=1)
            s = lax.dot_general(kg, q4, NT, preferred_element_type=f32) * (SCALE * LOG2E) + b4
            top = jnp.max(s, axis=0, keepdims=True)
            p = jnp.exp2(s - top)
            p = p * (1.0 / jnp.sum(p, axis=0, keepdims=True))
            dp = lax.dot_general(vg, do4, NT, preferred_element_type=f32)
            ds = (p * (dp - dots)).astype(bf16)
            dq = lax.dot_general(ds, kg, TN, preferred_element_type=f32) * SCALE
            for b in range(HB):
                dq_ref[:, cols[b]] = dq[b * ROWS : (b + 1) * ROWS, :].astype(bf16)
            dk_acc = dk_acc + jnp.dot(ds, q4, preferred_element_type=f32)
            dv_acc = dv_acc + jnp.dot(p.astype(bf16), do4, preferred_element_type=f32)
            return dk_acc, dv_acc

        zero = jnp.zeros((total, HD), f32)
        dk_acc, dv_acc = lax.fori_loop(0, HG // HB, heads, (zero, zero))
        dk = (dk_acc * SCALE).astype(bf16)
        dv = dv_acc.astype(bf16)
        spread = jnp.dot(
            put[:, 0:width],
            jnp.concatenate([dk[ROWS:], dv[ROWS:]], axis=1),
            preferred_element_type=f32,
        ).astype(bf16)
        dkv_ref[0] = spread[:, :HD]
        dkv_ref[1] = spread[:, HD:]
        dkv_ref[0, pl.ds(pl.multiple_of(first, ROWS), ROWS), :] = dk[:ROWS]
        dkv_ref[1, pl.ds(pl.multiple_of(first, ROWS), ROWS), :] = dv[:ROWS]

    lower = -1
    for width in WIDTHS:
        pl.when((n_far > lower) & (n_far <= width))(functools.partial(run, width))
        lower = width


def attention(queries, grad_out, saved_out, key_group, value_group, subtree_end):
    place = lax.axis_index("tensor").astype(jnp.int32).reshape(1)
    wide = pl.BlockSpec((ROWS, HG * HD), lambda g, place: (0, g))
    whole = pl.BlockSpec((SEQ, KVH * HD), lambda g, place: (0, 0))
    part = pl.BlockSpec((2, SEQ, HD), lambda g, place: (0, 0, g))
    far_most = SEQ - ROWS
    return pl.pallas_call(
        attention_kernel,
        grid_spec=pltpu.PrefetchScalarGridSpec(
            num_scalar_prefetch=1,
            grid=(KVH,),
            in_specs=[
                pl.BlockSpec((BLOCKS, ROWS), lambda g, place: (0, 0)),
                wide, wide, wide, whole, whole,
            ],
            out_specs=[wide, part],
            scratch_shapes=[
                pltpu.VMEM((BLOCKS, ROWS), jnp.int32),
                pltpu.VMEM((far_most, SEQ), bf16),
                pltpu.VMEM((SEQ, far_most), bf16),
                pltpu.VMEM((SEQ, ROWS), f32),
                pltpu.VMEM((SEQ, KVH * HD), bf16),
                pltpu.VMEM((SEQ, KVH * HD), bf16),
            ],
        ),
        out_shape=[
            jax.ShapeDtypeStruct((ROWS, HQ * HD), bf16),
            jax.ShapeDtypeStruct((2, SEQ, KVH * HD), bf16),
        ],
        compiler_params=pltpu.CompilerParams(vmem_limit_bytes=61 * 1024 * 1024),
    )(place, subtree_end.reshape(BLOCKS, ROWS), queries, grad_out, saved_out, key_group, value_group)


MESH = pl.DeviceIdType.MESH
KV = KVH * HD
FEAT = 2048
ORDER = (1, 3, 2)


def coords():
    d, t = lax.axis_index("dp"), lax.axis_index("tensor")
    return d // 4, d % 4, t // 4, (t // 2) % 2, t % 2


def device(yh, x, z, yl, c):
    return (yh * 4 + x, z * 4 + yl * 2 + c)


def greet(peers):
    barrier = pltpu.get_barrier_semaphore()
    for peer in peers:
        pl.semaphore_signal(barrier, inc=1, device_id=peer, device_id_type=MESH)
    pl.semaphore_wait(barrier, len(peers))


class Sender:
    def __init__(self, send_sem, recv_sem):
        self.sems, self.all = (send_sem, recv_sem), []

    def __call__(self, src, dst, peer):
        i = len(self.all)
        copy = pltpu.make_async_remote_copy(
            src_ref=src, dst_ref=dst, send_sem=self.sems[0].at[i], recv_sem=self.sems[1].at[i],
            device_id=peer, device_id_type=MESH,
        )
        copy.start()
        self.all.append(copy)
        return copy

    def finish(self):
        for copy in self.all:
            copy.wait_send()


GATHER_COPIES = 42


def gather_kernel(k_ref, v_ref, n_ref, k_all, v_all, cols, send_sem, recv_sem, local_sem):
    yh, x, z, yl, c = coords()
    y_peer = device(yh, x, z, 1 - yl, c)
    core_peer = device(yh, x, z, yl, 1 - c)
    z_peer = {d: device(yh, x, (z + d) % 4, yl, c) for d in (1, 2, 3)}
    x_peer = {d: device(yh, (x + d) % 4, z, yl, c) for d in ORDER}
    greet([y_peer, core_peer, *z_peer.values(), *x_peer.values()])
    send = Sender(send_sem, recv_sem)

    def rows(zz, yy):
        return pl.ds(pl.multiple_of((zz * 4 + yy * 2 + c) * ROWS, ROWS), ROWS)

    def columns(part, xx):
        return pl.ds(pl.multiple_of(part * (D // 2) + xx * 1024, 1024), 1024)

    mine = rows(z, yl)
    first = send(k_ref, k_all.at[mine], y_peer)
    k_z = {d: send(k_ref, k_all.at[mine], z_peer[d]) for d in ORDER}
    v_z = {d: send(v_ref, v_all.at[mine], z_peer[d]) for d in ORDER}
    v_y = send(v_ref, v_all.at[mine], y_peer)
    n_x = {}
    for d in ORDER:
        for part in (0, 1):
            n_x[d, part] = send(
                n_ref.at[:, columns(part, (x + d) % 4)],
                cols.at[4 - d, c, :, pl.ds(part * 1024, 1024)],
                x_peer[d],
            )
    local = [
        pltpu.make_async_copy(k_ref, k_all.at[mine], local_sem.at[0]),
        pltpu.make_async_copy(v_ref, v_all.at[mine], local_sem.at[1]),
    ]
    for part in (0, 1):
        local.append(
            pltpu.make_async_copy(
                n_ref.at[:, columns(part, x)],
                cols.at[0, c, :, pl.ds(part * 1024, 1024)],
                local_sem.at[2 + part],
            )
        )
    for copy in local:
        copy.start()
    crossed = [send(k_ref, k_all.at[mine], core_peer), send(v_ref, v_all.at[mine], core_peer)]
    for part in (0, 1):
        crossed.append(
            send(
                n_ref.at[:, columns(part, x)],
                cols.at[0, c, :, pl.ds(part * 1024, 1024)],
                core_peer,
            )
        )

    def cross(whole, zz, yy):
        crossed.append(send(whole.at[rows(zz, yy)], whole.at[rows(zz, yy)], core_peer))

    first.wait_recv()
    other = rows(z, 1 - yl)
    k_yz = {d: send(k_all.at[other], k_all.at[other], z_peer[d]) for d in ORDER}
    cross(k_all, z, 1 - yl)
    v_zy = {}
    for d in ORDER:
        from_z = (z + 4 - d) % 4
        v_z[d].wait_recv()
        v_zy[d] = send(v_all.at[rows(from_z, yl)], v_all.at[rows(from_z, yl)], y_peer)
        cross(v_all, from_z, yl)
    for d in ORDER:
        k_z[d].wait_recv()
        cross(k_all, (z + 4 - d) % 4, yl)
    v_y.wait_recv()
    cross(v_all, z, 1 - yl)
    for d in ORDER:
        k_yz[d].wait_recv()
        cross(k_all, (z + 4 - d) % 4, 1 - yl)
    for d in ORDER:
        v_zy[d].wait_recv()
        cross(v_all, (z + 4 - d) % 4, 1 - yl)
    for d in ORDER:
        for part in (0, 1):
            n_x[d, part].wait_recv()
        place = cols.at[4 - d, c]
        crossed.append(send(place, place, core_peer))
    for copy in crossed:
        copy.wait_recv()
    for copy in local:
        copy.wait()
    send.finish()


def gather(keys, values, normed_input):
    return pl.pallas_call(
        gather_kernel,
        in_specs=[pl.BlockSpec(memory_space=pl.ANY)] * 3,
        out_specs=[pl.BlockSpec(memory_space=pl.ANY)] * 3,
        out_shape=[
            jax.ShapeDtypeStruct((SEQ, KV), bf16),
            jax.ShapeDtypeStruct((SEQ, KV), bf16),
            jax.ShapeDtypeStruct((4, 2, ROWS, FEAT), bf16),
        ],
        scratch_shapes=[
            pltpu.SemaphoreType.DMA((GATHER_COPIES,)),
            pltpu.SemaphoreType.DMA((GATHER_COPIES,)),
            pltpu.SemaphoreType.DMA((4,)),
        ],
        compiler_params=pltpu.CompilerParams(
            collective_id=0, has_side_effects=True, vmem_limit_bytes=61 * 1024 * 1024
        ),
    )(keys, values, normed_input)


SUM_COPIES = 80
PARTS = 2
WIDE = KV // PARTS
HALF = WIDE // 2
SOON = (1, 3, 2, 0)


def sum_kernel(
    part_ref, cols_ref, gk_ref, gv_ref, wk_ref, wv_ref,
    cols, own, came, a1, b1, a1_in, b1_in, b2, b2_in, a2, a2_in, grads, g_in,
    wa, wb, wa_in, wb_in, wa2, wb2, wa2_in, wb2_in, w_own, w_in,
    send_sem, recv_sem, local_sem,
):
    yh, x, z, yl, c = coords()
    y = yh * 2 + yl
    y_peer = device(yh, x, z, 1 - yl, c)
    core_peer = device(yh, x, z, yl, 1 - c)
    z_at = {d: (z + d) % 4 for d in range(4)}
    y_at = {d: (y + d) % 4 for d in range(4)}
    z_peer = {d: device(yh, x, z_at[d], yl, c) for d in ORDER}
    y_ring = {d: device(y_at[d] // 2, x, z, y_at[d] % 2, c) for d in ORDER}
    x_peer = {d: device(yh, (x + d) % 4, z, yl, c) for d in ORDER}
    greet([core_peer, *z_peer.values(), *y_ring.values(), *x_peer.values()])
    send = Sender(send_sem, recv_sem)
    is_key = c == 0
    theirs = pl.ds(pl.multiple_of((1 - c) * ROWS, ROWS), ROWS)
    ours = pl.ds(pl.multiple_of(c * ROWS, ROWS), ROWS)
    local, cross, a_z, b_y, b_z, a_y, g_x = {}, {}, {}, {}, {}, {}, {}
    w_a, w_b, w_ay, w_bz = {}, {}, {}, {}

    for i, d in enumerate(SOON):
        local[d] = pltpu.make_async_copy(part_ref.at[c, z_at[d]], own.at[z_at[d]], local_sem.at[i])
        local[d].start()
    for h in range(PARTS):
        for d in SOON:
            strip = pl.ds(h * WIDE, WIDE)
            cross[h, d] = send(
                part_ref.at[1 - c, z_at[d], :, :, strip],
                came.at[z_at[d], :, :, strip],
                core_peer,
            )
    brought = pltpu.make_async_copy(cols_ref, cols, local_sem.at[4])
    brought.start()

    def scatter(h):
        for d in SOON:
            at = z_at[d]
            cross[h, d].wait_recv()
            if h == 0:
                local[d].wait()
            for yy in (0, 1):
                strip = slice(h * WIDE, (h + 1) * WIDE)
                total = own[at, yy, :, strip].astype(f32) + came[at, yy, :, strip].astype(f32)
                a1[h, at, yy] = total[:, :HALF].astype(bf16)
                b1[h, at, yy] = total[:, HALF:].astype(bf16)
            if d:
                a_z[h, d] = send(a1.at[h, at], a1_in.at[h, d - 1], z_peer[d])
            b_y[h, d] = send(b1.at[h, at, 1 - yl], b1_in.at[h, at], y_peer)

    def right_turn(h):
        for d in ORDER:
            at = z_at[d]
            b_y[h, d].wait_recv()
            b2[h, d - 1] = (b1[h, at, yl].astype(f32) + b1_in[h, at].astype(f32)).astype(bf16)
            b_z[h, d] = send(b2.at[h, d - 1], b2_in.at[h, d - 1], z_peer[d])

    def left(h, yy):
        total = a1[h, z, yy].astype(f32)
        for d in ORDER:
            total = total + a1_in[h, d - 1, yy].astype(f32)
        return total

    def left_turn(h):
        for d in ORDER:
            a_z[h, d].wait_recv()
        a2[h] = left(h, 1 - yl).astype(bf16)
        a_y[h] = send(a2.at[h], a2_in.at[h], y_peer)

    def spread(h):
        b_y[h, 0].wait_recv()
        total = b1[h, z, yl].astype(f32) + b1_in[h, z].astype(f32)
        for d in ORDER:
            b_z[h, d].wait_recv()
            total = total + b2_in[h, d - 1].astype(f32)
        grads[h, 0, :, HALF:] = total.astype(bf16)
        kept = left(h, yl)
        a_y[h].wait_recv()
        grads[h, 0, :, :HALF] = (kept + a2_in[h].astype(f32)).astype(bf16)
        for d in ORDER:
            g_x[h, d] = send(grads.at[h, 0], grads.at[h, 4 - d], x_peer[d])
        g_x[h, 0] = send(grads.at[h, 0, theirs], g_in.at[h], core_peer)

    def first_outputs():
        for h in range(PARTS):
            g_x[h, 0].wait_recv()
            mine, other = grads[h, 0, ours, :].astype(f32), g_in[h].astype(f32)
            strip = slice(h * WIDE, (h + 1) * WIDE)
            gk_ref[:, strip] = jnp.where(is_key, mine, other).astype(bf16)
            gv_ref[:, strip] = jnp.where(is_key, other, mine).astype(bf16)

    def project(h):
        for d in ORDER:
            g_x[h, d].wait_recv()
        if h == 0:
            brought.wait()
        right_side = grads[h].reshape(4 * 2 * ROWS, WIDE)
        for d in SOON:
            at = z_at[d]
            for top in (0, 1):
                start = pl.multiple_of(top * 1024 + at * 256, 256)
                left_side = cols[:, :, :, pl.ds(start, 256)].reshape(4 * 2 * ROWS, 256)
                block = lax.dot_general(left_side, right_side, TN, preferred_element_type=f32)
                block = block.astype(bf16)
                for low in (0, 1):
                    piece = block[low * ROWS : (low + 1) * ROWS]
                    wa[h, at, top * 2 + low] = piece[:, :HALF]
                    wb[h, top * 2 + low, at] = piece[:, HALF:]
            if d:
                w_a[h, d] = send(wa.at[h, at], wa_in.at[h, d - 1], z_peer[d])
        for d in ORDER:
            w_b[h, d] = send(wb.at[h, y_at[d]], wb_in.at[h, d - 1], y_ring[d])

    def over_z(h, yy):
        total = wa[h, z, yy].astype(f32)
        for d in ORDER:
            total = total + wa_in[h, d - 1, yy].astype(f32)
        return total

    def over_y(h, zz):
        total = wb[h, y, zz].astype(f32)
        for d in ORDER:
            total = total + wb_in[h, d - 1, zz].astype(f32)
        return total

    def turn(h):
        for d in ORDER:
            w_a[h, d].wait_recv()
        for d in ORDER:
            wa2[h, d - 1] = over_z(h, y_at[d]).astype(bf16)
            w_ay[h, d] = send(wa2.at[h, d - 1], wa2_in.at[h, d - 1], y_ring[d])
        for d in ORDER:
            w_b[h, d].wait_recv()
        for d in ORDER:
            wb2[h, d - 1] = over_y(h, z_at[d]).astype(bf16)
            w_bz[h, d] = send(wb2.at[h, d - 1], wb2_in.at[h, d - 1], z_peer[d])

    w_core = {}

    def finish(h):
        total = over_z(h, y)
        for d in ORDER:
            w_ay[h, d].wait_recv()
            total = total + wa2_in[h, d - 1].astype(f32)
        w_own[h, :, :HALF] = total
        total = over_y(h, z)
        for d in ORDER:
            w_bz[h, d].wait_recv()
            total = total + wb2_in[h, d - 1].astype(f32)
        w_own[h, :, HALF:] = total
        out = pl.ds(pl.multiple_of((1 - c) * 64, 64), 64)
        w_core[h] = send(w_own.at[h, out], w_in.at[h], core_peer)

    def last_outputs(h):
        mine = w_own[h, pl.ds(pl.multiple_of(c * 64, 64), 64), :]
        w_core[h].wait_recv()
        other = w_in[h]
        strip = slice(h * WIDE, (h + 1) * WIDE)
        wk_ref[:, strip] = jnp.where(is_key, mine, other)
        wv_ref[:, strip] = jnp.where(is_key, other, mine)

    scatter(0)
    right_turn(0)
    scatter(1)
    left_turn(0)
    spread(0)
    right_turn(1)
    left_turn(1)
    spread(1)
    first_outputs()
    for step in (project, turn, finish):
        for h in range(PARTS):
            step(h)
    for h in range(PARTS):
        last_outputs(h)
    send.finish()


def sums(parts, cols):
    vmem = lambda *shape: pltpu.VMEM(shape, bf16)
    anywhere = pl.BlockSpec(memory_space=pl.ANY)
    inside = pl.BlockSpec(memory_space=pltpu.VMEM)
    R2 = 2 * ROWS
    return pl.pallas_call(
        sum_kernel,
        in_specs=[anywhere] * 2,
        out_specs=[inside] * 4,
        out_shape=[
            jax.ShapeDtypeStruct((ROWS, KV), bf16),
            jax.ShapeDtypeStruct((ROWS, KV), bf16),
            jax.ShapeDtypeStruct((64, KV), f32),
            jax.ShapeDtypeStruct((64, KV), f32),
        ],
        scratch_shapes=[
            vmem(4, 2, ROWS, FEAT),
            vmem(4, 2, R2, KV),
            vmem(4, 2, R2, KV),
            vmem(PARTS, 4, 2, R2, HALF),
            vmem(PARTS, 4, 2, R2, HALF),
            vmem(PARTS, 3, 2, R2, HALF),
            vmem(PARTS, 4, R2, HALF),
            vmem(PARTS, 3, R2, HALF),
            vmem(PARTS, 3, R2, HALF),
            vmem(PARTS, R2, HALF),
            vmem(PARTS, R2, HALF),
            vmem(PARTS, 4, R2, WIDE),
            vmem(PARTS, ROWS, WIDE),
            vmem(PARTS, 4, 4, ROWS, HALF),
            vmem(PARTS, 4, 4, ROWS, HALF),
            vmem(PARTS, 3, 4, ROWS, HALF),
            vmem(PARTS, 3, 4, ROWS, HALF),
            vmem(PARTS, 3, ROWS, HALF),
            vmem(PARTS, 3, ROWS, HALF),
            vmem(PARTS, 3, ROWS, HALF),
            vmem(PARTS, 3, ROWS, HALF),
            pltpu.VMEM((PARTS, ROWS, WIDE), f32),
            pltpu.VMEM((PARTS, 64, WIDE), f32),
            pltpu.SemaphoreType.DMA((SUM_COPIES,)),
            pltpu.SemaphoreType.DMA((SUM_COPIES,)),
            pltpu.SemaphoreType.DMA((5,)),
        ],
        compiler_params=pltpu.CompilerParams(
            collective_id=1, has_side_effects=True, vmem_limit_bytes=61 * 1024 * 1024
        ),
    )(parts.reshape(2, 4, 2, R2, KV), cols)


def settle_kernel(*refs):
    for source, target in zip(refs[:4], refs[4:]):
        target[...] = source[...]


def settle(results):
    inside = pl.BlockSpec(memory_space=pltpu.VMEM)
    return pl.pallas_call(
        settle_kernel,
        in_specs=[inside] * 4,
        out_specs=[inside] * 4,
        out_shape=[jax.ShapeDtypeStruct(r.shape, r.dtype) for r in results],
        compiler_params=pltpu.CompilerParams(vmem_limit_bytes=61 * 1024 * 1024),
    )(*results)


def shards(queries, keys, values, saved_out, grad_out, normed_input, subtree_end):
    key_group, value_group, cols = gather(keys, values, normed_input)
    grad_queries, parts = attention(
        queries, grad_out, saved_out, key_group, value_group, subtree_end
    )
    return (grad_queries, *settle(sums(parts, cols)))


def solution(mesh):
    rows = P(("dp", "tensor"), None)
    return jax.shard_map(
        shards, mesh=mesh, in_specs=(rows,) * 6 + (P("dp"),), out_specs=(rows,) * 5, check_vma=False
    )
```

```python
import functools

import jax
import jax.numpy as jnp
from jax import lax
from jax.experimental import pallas as pl
from jax.experimental.pallas import tpu as pltpu
from jax.sharding import PartitionSpec as P

D = 8192
HQ = 64
KVH = 4
HD = 128
SEQ = 2048
ROWS = 128
BLOCKS = SEQ // ROWS
HG = HQ // KVH
HB = 8
WIDTHS = (128, 256, 512, SEQ - ROWS)
SCALE = HD ** (-0.5)
LOG2E = 1.4426950408889634
NT = (((1,), (1,)), ((), ()))
TN = (((0,), (0,)), ((), ()))
f32 = jnp.float32
bf16 = jnp.bfloat16


def attention_kernel(
    place_ref, end_ref, q_ref, do_ref, o_ref, k_ref, v_ref,
    dq_ref, dkv_ref, rank, pick, put, bias, kc, vc,
):
    t = place_ref[0]
    g = pl.program_id(0)
    first = t * ROWS
    lane = lax.broadcasted_iota(jnp.int32, (ROWS, ROWS), 1)
    sub = lax.broadcasted_iota(jnp.int32, (ROWS, ROWS), 0)

    pos = (
        lax.broadcasted_iota(jnp.int32, (BLOCKS, ROWS), 0) * ROWS
        + lax.broadcasted_iota(jnp.int32, (BLOCKS, ROWS), 1)
    )
    far = (pos < first) & (end_ref[...] >= first)
    n_far = jnp.sum(far.astype(jnp.int32))

    @pl.when(g == 0)
    def _prepare():
        flags = far.astype(f32).astype(bf16)
        upto = (sub <= lane).astype(f32).astype(bf16)
        within = jnp.dot(flags, upto, preferred_element_type=f32)
        totals = jnp.dot(flags, jnp.ones((ROWS, ROWS), bf16), preferred_element_type=f32)
        earlier = (
            lax.broadcasted_iota(jnp.int32, (BLOCKS, BLOCKS), 1)
            < lax.broadcasted_iota(jnp.int32, (BLOCKS, BLOCKS), 0)
        )
        before = jnp.dot(
            earlier.astype(f32).astype(bf16), totals.astype(bf16), preferred_element_type=f32
        )
        rank[...] = jnp.where(far, (within + before).astype(jnp.int32) - 1, -1)
        own_end = end_ref[pl.ds(t, 1), :]
        end_col = jnp.sum(jnp.where(sub == lane, own_end, 0), axis=1, keepdims=True)
        ok = (sub <= lane) & (lane + first <= end_col)
        bias[0:ROWS, :] = jnp.where(ok, 0.0, -1e30)
        kc[0:ROWS, :] = k_ref[pl.ds(pl.multiple_of(first, ROWS), ROWS), :]
        vc[0:ROWS, :] = v_ref[pl.ds(pl.multiple_of(first, ROWS), ROWS), :]

    def run(width):
        total = width + ROWS
        heads_each = HB if width <= 4 * ROWS else 2

        @pl.when(g == 0)
        def _compact():
            def one(b, carry):
                at = pl.multiple_of(b * ROWS, ROWS)
                end_sum = jnp.zeros((ROWS, ROWS), jnp.int32)
                for r in range(BLOCKS):
                    column = jnp.sum(
                        jnp.where(sub == lane, rank[r : r + 1, :], 0), axis=1, keepdims=True
                    )
                    put[r * ROWS : (r + 1) * ROWS, pl.ds(at, ROWS)] = (
                        (column == lane + at).astype(f32).astype(bf16)
                    )
                    hit = rank[r : r + 1, :] == sub + at
                    end_sum = end_sum + jnp.where(hit, end_ref[r : r + 1, :] + 1, 0)
                    pick[pl.ds(at, ROWS), r * ROWS : (r + 1) * ROWS] = hit.astype(f32).astype(bf16)
                end_col = jnp.sum(end_sum, axis=1, keepdims=True) - 1
                bias[pl.ds(at + ROWS, ROWS), :] = jnp.where(lane + first <= end_col, 0.0, -1e30)
                chosen = pick[pl.ds(at, ROWS), :]
                kc[pl.ds(at + ROWS, ROWS), :] = jnp.dot(
                    chosen, k_ref[...], preferred_element_type=f32
                ).astype(bf16)
                vc[pl.ds(at + ROWS, ROWS), :] = jnp.dot(
                    chosen, v_ref[...], preferred_element_type=f32
                ).astype(bf16)
                return carry

            lax.fori_loop(0, width // ROWS, one, 0)

        gcol = pl.multiple_of(g * HD, HD)
        kg = kc[0:total, pl.ds(gcol, HD)]
        vg = vc[0:total, pl.ds(gcol, HD)]

        def heads(i, acc):
            dk_acc, dv_acc = acc
            cols = [pl.ds(pl.multiple_of((i * heads_each + b) * HD, HD), HD) for b in range(heads_each)]
            q4 = jnp.concatenate([q_ref[:, c] for c in cols], axis=0)
            do4 = jnp.concatenate([do_ref[:, c] for c in cols], axis=0)
            o4 = jnp.concatenate([o_ref[:, c] for c in cols], axis=0)
            prod = do4.astype(f32) * o4.astype(f32)
            high = prod.astype(bf16)
            low = (prod - high.astype(f32)).astype(bf16)
            ones = jnp.ones((16, HD), bf16)
            dots = (
                lax.dot_general(ones, high, NT, preferred_element_type=f32)
                + lax.dot_general(ones, low, NT, preferred_element_type=f32)
            )[0:1, :]
            b1 = bias[0:total, :]
            b4 = jnp.concatenate([b1] * heads_each, axis=1)
            s = lax.dot_general(kg, q4, NT, preferred_element_type=f32) * (SCALE * LOG2E) + b4
            top = jnp.max(s, axis=0, keepdims=True)
            p = jnp.exp2(s - top)
            p = p * (1.0 / jnp.sum(p, axis=0, keepdims=True))
            dp = lax.dot_general(vg, do4, NT, preferred_element_type=f32)
            ds = (p * (dp - dots)).astype(bf16)
            dq = lax.dot_general(ds, kg, TN, preferred_element_type=f32) * SCALE
            for b in range(heads_each):
                dq_ref[:, cols[b]] = dq[b * ROWS : (b + 1) * ROWS, :].astype(bf16)
            dk_acc = dk_acc + jnp.dot(ds, q4, preferred_element_type=f32)
            dv_acc = dv_acc + jnp.dot(p.astype(bf16), do4, preferred_element_type=f32)
            return dk_acc, dv_acc

        zero = jnp.zeros((total, HD), f32)
        dk_acc, dv_acc = lax.fori_loop(0, HG // heads_each, heads, (zero, zero))
        dk = (dk_acc * SCALE).astype(bf16)
        dv = dv_acc.astype(bf16)
        spread = jnp.dot(
            put[:, 0:width],
            jnp.concatenate([dk[ROWS:], dv[ROWS:]], axis=1),
            preferred_element_type=f32,
        ).astype(bf16)
        dkv_ref[0] = spread[:, :HD]
        dkv_ref[1] = spread[:, HD:]
        dkv_ref[0, pl.ds(pl.multiple_of(first, ROWS), ROWS), :] = dk[:ROWS]
        dkv_ref[1, pl.ds(pl.multiple_of(first, ROWS), ROWS), :] = dv[:ROWS]

    lower = -1
    for width in WIDTHS:
        pl.when((n_far > lower) & (n_far <= width))(functools.partial(run, width))
        lower = width


def attention(queries, grad_out, saved_out, key_group, value_group, subtree_end):
    place = lax.axis_index("tensor").astype(jnp.int32).reshape(1)
    wide = pl.BlockSpec((ROWS, HG * HD), lambda g, place: (0, g))
    whole = pl.BlockSpec((SEQ, KVH * HD), lambda g, place: (0, 0))
    part = pl.BlockSpec((2, SEQ, HD), lambda g, place: (0, 0, g))
    far_most = SEQ - ROWS
    return pl.pallas_call(
        attention_kernel,
        grid_spec=pltpu.PrefetchScalarGridSpec(
            num_scalar_prefetch=1,
            grid=(KVH,),
            in_specs=[
                pl.BlockSpec((BLOCKS, ROWS), lambda g, place: (0, 0)),
                wide, wide, wide, whole, whole,
            ],
            out_specs=[wide, part],
            scratch_shapes=[
                pltpu.VMEM((BLOCKS, ROWS), jnp.int32),
                pltpu.VMEM((far_most, SEQ), bf16),
                pltpu.VMEM((SEQ, far_most), bf16),
                pltpu.VMEM((SEQ, ROWS), f32),
                pltpu.VMEM((SEQ, KVH * HD), bf16),
                pltpu.VMEM((SEQ, KVH * HD), bf16),
            ],
        ),
        out_shape=[
            jax.ShapeDtypeStruct((ROWS, HQ * HD), bf16),
            jax.ShapeDtypeStruct((2, SEQ, KVH * HD), bf16),
        ],
        compiler_params=pltpu.CompilerParams(vmem_limit_bytes=61 * 1024 * 1024),
    )(place, subtree_end.reshape(BLOCKS, ROWS), queries, grad_out, saved_out, key_group, value_group)


MESH = pl.DeviceIdType.MESH
KV = KVH * HD
FEAT = 2048
ORDER = (1, 3, 2)


def coords():
    d, t = lax.axis_index("dp"), lax.axis_index("tensor")
    return d // 4, d % 4, t // 4, (t // 2) % 2, t % 2


def device(yh, x, z, yl, c):
    return (yh * 4 + x, z * 4 + yl * 2 + c)


def greet(peers):
    barrier = pltpu.get_barrier_semaphore()
    for peer in peers:
        pl.semaphore_signal(barrier, inc=1, device_id=peer, device_id_type=MESH)
    pl.semaphore_wait(barrier, len(peers))


class Sender:
    def __init__(self, send_sem, recv_sem):
        self.sems, self.all = (send_sem, recv_sem), []

    def __call__(self, src, dst, peer):
        i = len(self.all)
        copy = pltpu.make_async_remote_copy(
            src_ref=src, dst_ref=dst, send_sem=self.sems[0].at[i], recv_sem=self.sems[1].at[i],
            device_id=peer, device_id_type=MESH,
        )
        copy.start()
        self.all.append(copy)
        return copy

    def finish(self):
        for copy in self.all:
            copy.wait_send()


GATHER_COPIES = 42


def gather_kernel(k_ref, v_ref, n_ref, k_all, v_all, cols, send_sem, recv_sem, local_sem):
    yh, x, z, yl, c = coords()
    y_peer = device(yh, x, z, 1 - yl, c)
    core_peer = device(yh, x, z, yl, 1 - c)
    z_peer = {d: device(yh, x, (z + d) % 4, yl, c) for d in (1, 2, 3)}
    x_peer = {d: device(yh, (x + d) % 4, z, yl, c) for d in ORDER}
    greet([y_peer, core_peer, *z_peer.values(), *x_peer.values()])
    send = Sender(send_sem, recv_sem)

    def rows(zz, yy):
        return pl.ds(pl.multiple_of((zz * 4 + yy * 2 + c) * ROWS, ROWS), ROWS)

    def columns(part, xx):
        return pl.ds(pl.multiple_of(part * (D // 2) + xx * 1024, 1024), 1024)

    mine = rows(z, yl)
    first = send(k_ref, k_all.at[mine], y_peer)
    k_z = {d: send(k_ref, k_all.at[mine], z_peer[d]) for d in ORDER}
    v_z = {d: send(v_ref, v_all.at[mine], z_peer[d]) for d in ORDER}
    v_y = send(v_ref, v_all.at[mine], y_peer)
    n_x = {}
    for d in ORDER:
        for part in (0, 1):
            n_x[d, part] = send(
                n_ref.at[:, columns(part, (x + d) % 4)],
                cols.at[4 - d, c, :, pl.ds(part * 1024, 1024)],
                x_peer[d],
            )
    local = [
        pltpu.make_async_copy(k_ref, k_all.at[mine], local_sem.at[0]),
        pltpu.make_async_copy(v_ref, v_all.at[mine], local_sem.at[1]),
    ]
    for part in (0, 1):
        local.append(
            pltpu.make_async_copy(
                n_ref.at[:, columns(part, x)],
                cols.at[0, c, :, pl.ds(part * 1024, 1024)],
                local_sem.at[2 + part],
            )
        )
    for copy in local:
        copy.start()
    crossed = [send(k_ref, k_all.at[mine], core_peer), send(v_ref, v_all.at[mine], core_peer)]
    for part in (0, 1):
        crossed.append(
            send(
                n_ref.at[:, columns(part, x)],
                cols.at[0, c, :, pl.ds(part * 1024, 1024)],
                core_peer,
            )
        )

    def cross(whole, zz, yy):
        crossed.append(send(whole.at[rows(zz, yy)], whole.at[rows(zz, yy)], core_peer))

    first.wait_recv()
    other = rows(z, 1 - yl)
    k_yz = {d: send(k_all.at[other], k_all.at[other], z_peer[d]) for d in ORDER}
    cross(k_all, z, 1 - yl)
    v_zy = {}
    for d in ORDER:
        from_z = (z + 4 - d) % 4
        v_z[d].wait_recv()
        v_zy[d] = send(v_all.at[rows(from_z, yl)], v_all.at[rows(from_z, yl)], y_peer)
        cross(v_all, from_z, yl)
    for d in ORDER:
        k_z[d].wait_recv()
        cross(k_all, (z + 4 - d) % 4, yl)
    v_y.wait_recv()
    cross(v_all, z, 1 - yl)
    for d in ORDER:
        k_yz[d].wait_recv()
        cross(k_all, (z + 4 - d) % 4, 1 - yl)
    for d in ORDER:
        v_zy[d].wait_recv()
        cross(v_all, (z + 4 - d) % 4, 1 - yl)
    for d in ORDER:
        for part in (0, 1):
            n_x[d, part].wait_recv()
        place = cols.at[4 - d, c]
        crossed.append(send(place, place, core_peer))
    for copy in crossed:
        copy.wait_recv()
    for copy in local:
        copy.wait()
    send.finish()


def gather(keys, values, normed_input):
    return pl.pallas_call(
        gather_kernel,
        in_specs=[pl.BlockSpec(memory_space=pl.ANY)] * 3,
        out_specs=[pl.BlockSpec(memory_space=pl.ANY)] * 3,
        out_shape=[
            jax.ShapeDtypeStruct((SEQ, KV), bf16),
            jax.ShapeDtypeStruct((SEQ, KV), bf16),
            jax.ShapeDtypeStruct((4, 2, ROWS, FEAT), bf16),
        ],
        scratch_shapes=[
            pltpu.SemaphoreType.DMA((GATHER_COPIES,)),
            pltpu.SemaphoreType.DMA((GATHER_COPIES,)),
            pltpu.SemaphoreType.DMA((4,)),
        ],
        compiler_params=pltpu.CompilerParams(
            collective_id=0, has_side_effects=True, vmem_limit_bytes=61 * 1024 * 1024
        ),
    )(keys, values, normed_input)


SUM_COPIES = 80
PARTS = 2
WIDE = KV // PARTS
HALF = WIDE // 2
SOON = (1, 3, 2, 0)


def sum_kernel(
    part_ref, cols_ref, gk_ref, gv_ref, wk_ref, wv_ref,
    cols, own, came, a1, b1, a1_in, b1_in, b2, b2_in, a2, a2_in, grads, g_in,
    wa, wb, wa_in, wb_in, wa2, wb2, wa2_in, wb2_in, w_own, w_in,
    send_sem, recv_sem, local_sem,
):
    yh, x, z, yl, c = coords()
    y = yh * 2 + yl
    y_peer = device(yh, x, z, 1 - yl, c)
    core_peer = device(yh, x, z, yl, 1 - c)
    z_at = {d: (z + d) % 4 for d in range(4)}
    y_at = {d: (y + d) % 4 for d in range(4)}
    z_peer = {d: device(yh, x, z_at[d], yl, c) for d in ORDER}
    y_ring = {d: device(y_at[d] // 2, x, z, y_at[d] % 2, c) for d in ORDER}
    x_peer = {d: device(yh, (x + d) % 4, z, yl, c) for d in ORDER}
    greet([core_peer, *z_peer.values(), *y_ring.values(), *x_peer.values()])
    send = Sender(send_sem, recv_sem)
    is_key = c == 0
    theirs = pl.ds(pl.multiple_of((1 - c) * ROWS, ROWS), ROWS)
    ours = pl.ds(pl.multiple_of(c * ROWS, ROWS), ROWS)
    local, cross, a_z, b_y, b_z, a_y, g_x = {}, {}, {}, {}, {}, {}, {}
    w_a, w_b, w_ay, w_bz = {}, {}, {}, {}

    for i, d in enumerate(SOON):
        local[d] = pltpu.make_async_copy(part_ref.at[c, z_at[d]], own.at[z_at[d]], local_sem.at[i])
        local[d].start()
    for h in range(PARTS):
        for d in SOON:
            strip = pl.ds(h * WIDE, WIDE)
            cross[h, d] = send(
                part_ref.at[1 - c, z_at[d], :, :, strip],
                came.at[z_at[d], :, :, strip],
                core_peer,
            )
    brought = pltpu.make_async_copy(cols_ref, cols, local_sem.at[4])
    brought.start()

    def scatter(h):
        for d in SOON:
            at = z_at[d]
            cross[h, d].wait_recv()
            if h == 0:
                local[d].wait()
            for yy in (0, 1):
                strip = slice(h * WIDE, (h + 1) * WIDE)
                total = own[at, yy, :, strip].astype(f32) + came[at, yy, :, strip].astype(f32)
                a1[h, at, yy] = total[:, :HALF].astype(bf16)
                b1[h, at, yy] = total[:, HALF:].astype(bf16)
            if d:
                a_z[h, d] = send(a1.at[h, at], a1_in.at[h, d - 1], z_peer[d])
            b_y[h, d] = send(b1.at[h, at, 1 - yl], b1_in.at[h, at], y_peer)

    def right_turn(h):
        for d in ORDER:
            at = z_at[d]
            b_y[h, d].wait_recv()
            b2[h, d - 1] = (b1[h, at, yl].astype(f32) + b1_in[h, at].astype(f32)).astype(bf16)
            b_z[h, d] = send(b2.at[h, d - 1], b2_in.at[h, d - 1], z_peer[d])

    def left(h, yy):
        total = a1[h, z, yy].astype(f32)
        for d in ORDER:
            total = total + a1_in[h, d - 1, yy].astype(f32)
        return total

    def left_turn(h):
        for d in ORDER:
            a_z[h, d].wait_recv()
        a2[h] = left(h, 1 - yl).astype(bf16)
        a_y[h] = send(a2.at[h], a2_in.at[h], y_peer)

    def spread(h):
        b_y[h, 0].wait_recv()
        total = b1[h, z, yl].astype(f32) + b1_in[h, z].astype(f32)
        for d in ORDER:
            b_z[h, d].wait_recv()
            total = total + b2_in[h, d - 1].astype(f32)
        grads[h, 0, :, HALF:] = total.astype(bf16)
        kept = left(h, yl)
        a_y[h].wait_recv()
        grads[h, 0, :, :HALF] = (kept + a2_in[h].astype(f32)).astype(bf16)
        for d in ORDER:
            g_x[h, d] = send(grads.at[h, 0], grads.at[h, 4 - d], x_peer[d])
        g_x[h, 0] = send(grads.at[h, 0, theirs], g_in.at[h], core_peer)

    def first_outputs():
        for h in range(PARTS):
            g_x[h, 0].wait_recv()
            mine, other = grads[h, 0, ours, :].astype(f32), g_in[h].astype(f32)
            strip = slice(h * WIDE, (h + 1) * WIDE)
            gk_ref[:, strip] = jnp.where(is_key, mine, other).astype(bf16)
            gv_ref[:, strip] = jnp.where(is_key, other, mine).astype(bf16)

    def project(h):
        for d in ORDER:
            g_x[h, d].wait_recv()
        if h == 0:
            brought.wait()
        right_side = grads[h].reshape(4 * 2 * ROWS, WIDE)
        for d in SOON:
            at = z_at[d]
            for top in (0, 1):
                start = pl.multiple_of(top * 1024 + at * 256, 256)
                left_side = cols[:, :, :, pl.ds(start, 256)].reshape(4 * 2 * ROWS, 256)
                block = lax.dot_general(left_side, right_side, TN, preferred_element_type=f32)
                block = block.astype(bf16)
                for low in (0, 1):
                    piece = block[low * ROWS : (low + 1) * ROWS]
                    wa[h, at, top * 2 + low] = piece[:, :HALF]
                    wb[h, top * 2 + low, at] = piece[:, HALF:]
            if d:
                w_a[h, d] = send(wa.at[h, at], wa_in.at[h, d - 1], z_peer[d])
        for d in ORDER:
            w_b[h, d] = send(wb.at[h, y_at[d]], wb_in.at[h, d - 1], y_ring[d])

    def over_z(h, yy):
        total = wa[h, z, yy].astype(f32)
        for d in ORDER:
            total = total + wa_in[h, d - 1, yy].astype(f32)
        return total

    def over_y(h, zz):
        total = wb[h, y, zz].astype(f32)
        for d in ORDER:
            total = total + wb_in[h, d - 1, zz].astype(f32)
        return total

    def turn(h):
        for d in ORDER:
            w_a[h, d].wait_recv()
        for d in ORDER:
            wa2[h, d - 1] = over_z(h, y_at[d]).astype(bf16)
            w_ay[h, d] = send(wa2.at[h, d - 1], wa2_in.at[h, d - 1], y_ring[d])
        for d in ORDER:
            w_b[h, d].wait_recv()
        for d in ORDER:
            wb2[h, d - 1] = over_y(h, z_at[d]).astype(bf16)
            w_bz[h, d] = send(wb2.at[h, d - 1], wb2_in.at[h, d - 1], z_peer[d])

    w_core = {}

    def finish(h):
        total = over_z(h, y)
        for d in ORDER:
            w_ay[h, d].wait_recv()
            total = total + wa2_in[h, d - 1].astype(f32)
        w_own[h, :, :HALF] = total
        total = over_y(h, z)
        for d in ORDER:
            w_bz[h, d].wait_recv()
            total = total + wb2_in[h, d - 1].astype(f32)
        w_own[h, :, HALF:] = total
        out = pl.ds(pl.multiple_of((1 - c) * 64, 64), 64)
        w_core[h] = send(w_own.at[h, out], w_in.at[h], core_peer)

    def last_outputs(h):
        mine = w_own[h, pl.ds(pl.multiple_of(c * 64, 64), 64), :]
        w_core[h].wait_recv()
        other = w_in[h]
        strip = slice(h * WIDE, (h + 1) * WIDE)
        wk_ref[:, strip] = jnp.where(is_key, mine, other)
        wv_ref[:, strip] = jnp.where(is_key, other, mine)

    scatter(0)
    right_turn(0)
    scatter(1)
    left_turn(0)
    spread(0)
    right_turn(1)
    left_turn(1)
    spread(1)
    first_outputs()
    for step in (project, turn, finish):
        for h in range(PARTS):
            step(h)
    for h in range(PARTS):
        last_outputs(h)
    send.finish()


def sums(parts, cols):
    vmem = lambda *shape: pltpu.VMEM(shape, bf16)
    anywhere = pl.BlockSpec(memory_space=pl.ANY)
    inside = pl.BlockSpec(memory_space=pltpu.VMEM)
    R2 = 2 * ROWS
    return pl.pallas_call(
        sum_kernel,
        in_specs=[anywhere] * 2,
        out_specs=[inside] * 4,
        out_shape=[
            jax.ShapeDtypeStruct((ROWS, KV), bf16),
            jax.ShapeDtypeStruct((ROWS, KV), bf16),
            jax.ShapeDtypeStruct((64, KV), f32),
            jax.ShapeDtypeStruct((64, KV), f32),
        ],
        scratch_shapes=[
            vmem(4, 2, ROWS, FEAT),
            vmem(4, 2, R2, KV),
            vmem(4, 2, R2, KV),
            vmem(PARTS, 4, 2, R2, HALF),
            vmem(PARTS, 4, 2, R2, HALF),
            vmem(PARTS, 3, 2, R2, HALF),
            vmem(PARTS, 4, R2, HALF),
            vmem(PARTS, 3, R2, HALF),
            vmem(PARTS, 3, R2, HALF),
            vmem(PARTS, R2, HALF),
            vmem(PARTS, R2, HALF),
            vmem(PARTS, 4, R2, WIDE),
            vmem(PARTS, ROWS, WIDE),
            vmem(PARTS, 4, 4, ROWS, HALF),
            vmem(PARTS, 4, 4, ROWS, HALF),
            vmem(PARTS, 3, 4, ROWS, HALF),
            vmem(PARTS, 3, 4, ROWS, HALF),
            vmem(PARTS, 3, ROWS, HALF),
            vmem(PARTS, 3, ROWS, HALF),
            vmem(PARTS, 3, ROWS, HALF),
            vmem(PARTS, 3, ROWS, HALF),
            pltpu.VMEM((PARTS, ROWS, WIDE), f32),
            pltpu.VMEM((PARTS, 64, WIDE), f32),
            pltpu.SemaphoreType.DMA((SUM_COPIES,)),
            pltpu.SemaphoreType.DMA((SUM_COPIES,)),
            pltpu.SemaphoreType.DMA((5,)),
        ],
        compiler_params=pltpu.CompilerParams(
            collective_id=1, has_side_effects=True, vmem_limit_bytes=61 * 1024 * 1024
        ),
    )(parts.reshape(2, 4, 2, R2, KV), cols)


def settle_kernel(*refs):
    for source, target in zip(refs[:4], refs[4:]):
        target[...] = source[...]


def settle(results):
    inside = pl.BlockSpec(memory_space=pltpu.VMEM)
    return pl.pallas_call(
        settle_kernel,
        in_specs=[inside] * 4,
        out_specs=[inside] * 4,
        out_shape=[jax.ShapeDtypeStruct(r.shape, r.dtype) for r in results],
        compiler_params=pltpu.CompilerParams(vmem_limit_bytes=61 * 1024 * 1024),
    )(*results)


def shards(queries, keys, values, saved_out, grad_out, normed_input, subtree_end):
    key_group, value_group, cols = gather(keys, values, normed_input)
    grad_queries, parts = attention(
        queries, grad_out, saved_out, key_group, value_group, subtree_end
    )
    return (grad_queries, *settle(sums(parts, cols)))


def solution(mesh):
    rows = P(("dp", "tensor"), None)
    return jax.shard_map(
        shards, mesh=mesh, in_specs=(rows,) * 6 + (P("dp"),), out_specs=(rows,) * 5, check_vma=False
    )
```
